256 devices in a mesh: pipe: 8 (over x, core), ulys: 32 (over z, y).
Axes of the slice: x: 4, y: 4, z: 8, core: 2. Of those that a mesh axis runs over, the one named last changes fastest.
Arguments:
- activations: bfloat16 [8, 1024, 3072], P('pipe', 'ulys'), may hold values from -6 to 6
- patch_index: int32 [8], P('pipe'), may hold values from 0 to 11
- modulation: float32 [8, 3, 3072], P('pipe'), may hold values from -4 to 4
- qkv_weight: bfloat16 [8, 3072, 9216], P('pipe', None, 'ulys'), may hold values from -0.109375 to 0.109375
- out_weight: bfloat16 [8, 3072, 3072], P('pipe', 'ulys'), may hold values from -0.109375 to 0.109375
- stale_cache: bfloat16 [8, 32, 3072, 2, 384], P('pipe', 'ulys'), may hold values from -360 to 360
- id_cache: bfloat16 [8, 32, 6, 8, 2, 384], P('pipe', 'ulys'), may hold values from -360 to 360
- region_ids: int32 [8, 1024], P('pipe', 'ulys'), may hold values from 0 to 6
- id_counts: int32 [8, 6], P('pipe'), may hold values from 1 to 32, as said below
Outputs:
- next_activations: bfloat16 [8, 1024, 3072], P('pipe', 'ulys')
The draws below stay inside these ranges and needn't reach their ends.
Inputs may be any that keep to these rules, and one draw needn't show every extreme that they name: `id_counts`: in every section some subject has exactly 32 live identity tokens.
All inputs are finite; a program needn't handle non-finite values.
Results may differ from the reference program's by a relative error of at most 0.0117.
The reference program's roundings to bfloat16 on the way (of `hidden`, `fields` and `mixed`) count: a program that leaves them out, or rounds other values in their place, can miss the bound.
Values may be sent and summed in bfloat16 or wider, within the bound.
A program may use at most 128 MiB of HBM per device.

```python
import jax
import jax.numpy as jnp
from jax import lax

D = 3072
HEADS = 24
HD = 128
HPD = 3
GROUPS = 8
KSPLIT = 4
MB = 1024
PATCHES = 12
S = 12288
SUBJ = 6
IDTOK = 32
SECTIONS = 8
N_ULYS = 32


def draw_stale_cache(key, part):
    key = jax.random.fold_in(key, 11)
    shape = (SECTIONS, N_ULYS, S // KSPLIT, 2, HPD * HD)
    values = jnp.clip(jax.random.normal(key, shape, jnp.float32), -6.0, 6.0)
    return values.astype(jnp.bfloat16)


def draw_id_cache(key, part):
    key = jax.random.fold_in(key, 17)
    shape = (SECTIONS, N_ULYS, SUBJ, IDTOK // KSPLIT, 2, HPD * HD)
    values = jnp.clip(jax.random.normal(key, shape, jnp.float32), -6.0, 6.0)
    return values.astype(jnp.bfloat16)


def draw_id_counts(key, part):
    key = jax.random.fold_in(key, 23)
    first, second = jax.random.split(key)
    counts = jax.random.randint(first, (SECTIONS, SUBJ), 1, IDTOK + 1)
    chosen = jax.random.randint(second, (SECTIONS, 1), 0, SUBJ)
    hit = jnp.arange(SUBJ)[None, :] == chosen
    return jnp.where(hit, IDTOK, counts).astype(jnp.int32)


def with_ends(array, key, low, largest):
    place = [jax.random.randint(jax.random.fold_in(key, axis), (), 0, length) for axis, length in enumerate(array.shape)]
    longest = array.shape.index(max(array.shape))
    neighbour = place[:longest] + [(place[longest] + 1) % array.shape[longest]] + place[longest + 1:]
    return array.at[tuple(place)].set(low).at[tuple(neighbour)].set(largest)


def level_of(rng, shape, shards, smallest, high):
    loudness, own = 1.0, jax.random.fold_in(rng, 6)
    for dim, blocks in shards:
        steps = jnp.exp(jax.random.uniform(jax.random.fold_in(own, dim), (blocks,), jnp.float32, smallest / len(shards), high / len(shards)))
        loudness = loudness * jnp.repeat(steps, shape[dim] // blocks).reshape([-1 if axis == dim else 1 for axis in range(len(shape))])
    return loudness


def gaussian(stream_key, shape, deviation, most, cuts=(), kind=jnp.bfloat16):
    values = deviation * jax.random.normal(stream_key, shape, jnp.float32)
    if cuts:
        values = values * level_of(stream_key, shape, cuts, -0.22, 0.18)
    return jnp.clip(values, -most, most).astype(kind)


def setup_inputs(seed: int = 0) -> dict:
    key_list = jax.random.split(jax.random.key(seed), 10)
    activations = gaussian(key_list[0], (SECTIONS, MB, D), 1.0, 6.0, ((0, 8), (1, 32)))
    patch_index = with_ends(jax.random.randint(key_list[1], (SECTIONS,), 0, PATCHES), jax.random.fold_in(key_list[1], 1), 0, PATCHES - 1).astype(jnp.int32)
    modulation = gaussian(key_list[2], (SECTIONS, 3, D), 0.6, 4.0, ((0, 8),), jnp.float32)
    qkv_weight = gaussian(key_list[3], (SECTIONS, D, 3 * HEADS * HD), D ** -0.5, 0.109375, ((0, 8), (2, 32)))
    out_weight = gaussian(key_list[4], (SECTIONS, HEADS * HD, D), (HEADS * HD) ** -0.5, 0.109375, ((0, 8), (1, 32)))
    stale_cache = draw_stale_cache(jax.random.fold_in(key_list[9], 71), 0)
    id_cache = draw_id_cache(jax.random.fold_in(key_list[9], 71), 0)
    region_ids = with_ends(jax.random.randint(key_list[7], (SECTIONS, MB), 0, SUBJ + 1), jax.random.fold_in(key_list[7], 1), 0, SUBJ).astype(jnp.int32)
    id_counts = draw_id_counts(jax.random.fold_in(key_list[9], 71), 0)
    return {"activations": activations, "patch_index": patch_index, "modulation": modulation, "qkv_weight": qkv_weight, "out_weight": out_weight, "stale_cache": stale_cache, "id_cache": id_cache, "region_ids": region_ids, "id_counts": id_counts}


NEG_BIG = -1e+30

def section_pass(rows, modul, patch, qkv_w, out_w, cache, id_block, region, counts):
    lifted = rows.astype(jnp.float32)
    center = lax.optimization_barrier(jnp.mean(lifted, axis=1, keepdims=True))
    spread = lax.optimization_barrier(jnp.mean(jnp.square(lifted - center), axis=1, keepdims=True))
    normed = (lifted - center) * lax.rsqrt(spread + 1e-06)
    hidden = (normed * (1.0 + modul[1]) + modul[0]).astype(jnp.bfloat16)
    ordered = qkv_w.reshape(D, GROUPS, KSPLIT, 3, HPD, HD // KSPLIT).transpose(0, 3, 1, 4, 2, 5).reshape(D, 3 * HEADS * HD)
    fields = jnp.dot(hidden, ordered, preferred_element_type=jnp.float32).astype(jnp.bfloat16).reshape(MB, 3, HEADS, HD)
    queries = fields[:, 0].transpose(1, 0, 2)
    fresh_keys = fields[:, 1].transpose(1, 0, 2)
    fresh_values = fields[:, 2].transpose(1, 0, 2)
    stored = cache.reshape(GROUPS, KSPLIT, S // KSPLIT, 2, HPD, HD).transpose(3, 0, 4, 1, 2, 5).reshape(2, HEADS, S, HD)
    start = (patch * MB).astype(jnp.int32)
    zero = jnp.zeros((), jnp.int32)
    keys = lax.dynamic_update_slice(stored[0], fresh_keys, (zero, start, zero))
    values = lax.dynamic_update_slice(stored[1], fresh_values, (zero, start, zero))
    guests = id_block.reshape(GROUPS, KSPLIT, SUBJ, IDTOK // KSPLIT, 2, HPD, HD).transpose(4, 0, 5, 2, 1, 3, 6).reshape(2, HEADS, SUBJ * IDTOK, HD)
    slot = jnp.arange(IDTOK, dtype=jnp.int32)
    valid = slot[None, :] < counts[:, None]
    subject = jnp.arange(1, SUBJ + 1, dtype=jnp.int32)
    mask = ((region[:, None] == subject[None, :])[:, :, None] & valid[None]).reshape(MB, SUBJ * IDTOK)
    factor = HD ** (-0.5)

    def one_head(items):
        head_q, head_k, head_v, guest_k, guest_v = items
        scores = jnp.dot(head_q, head_k.T, preferred_element_type=jnp.float32) * factor
        peak = lax.optimization_barrier(jnp.max(scores, axis=1, keepdims=True))
        weights = jnp.exp(scores - peak)
        own = jnp.dot(weights.astype(jnp.bfloat16), head_v, preferred_element_type=jnp.float32) / lax.optimization_barrier(jnp.sum(weights, axis=1, keepdims=True))
        guest_scores = jnp.dot(head_q, guest_k.T, preferred_element_type=jnp.float32) * factor
        guest_peak = lax.optimization_barrier(jnp.max(jnp.where(mask, guest_scores, NEG_BIG), axis=1, keepdims=True))
        guest_weights = jnp.where(mask, jnp.exp(jnp.where(mask, guest_scores - guest_peak, 0.0)), 0.0)
        guest_total = jnp.maximum(lax.optimization_barrier(jnp.sum(guest_weights, axis=1, keepdims=True)), 1.0)
        guest = jnp.dot(guest_weights.astype(jnp.bfloat16), guest_v, preferred_element_type=jnp.float32) / guest_total
        return own + guest
    mixed = lax.map(one_head, (queries, keys, values, guests[0], guests[1]))
    mixed = mixed.transpose(1, 0, 2).reshape(MB, HEADS * HD).astype(jnp.bfloat16)
    out_ordered = out_w.reshape(GROUPS, KSPLIT, HPD, HD // KSPLIT, D).transpose(0, 2, 1, 3, 4).reshape(HEADS * HD, D)
    added = jnp.dot(mixed, out_ordered, preferred_element_type=jnp.float32)
    return (lifted + modul[2] * added).astype(jnp.bfloat16)

def reference(activations, patch_index, modulation, qkv_weight, out_weight, stale_cache, id_cache, region_ids, id_counts):
    results = []
    for section in range(SECTIONS):
        results.append(section_pass(activations[section], modulation[section], patch_index[section], qkv_weight[section], out_weight[section], stale_cache[section], id_cache[section], region_ids[section], id_counts[section]))
    return jnp.roll(jnp.stack(results), 1, axis=0)
```

```python
import functools

import jax
import jax.numpy as jnp
from jax import lax
from jax.experimental import pallas as pl
from jax.experimental.pallas import tpu as pltpu
from jax.sharding import PartitionSpec as P

MESH = pl.DeviceIdType.MESH
HD = 128
HPD = 3
NZ = 8
NY = 4
SUBJ = 6
NEG_BIG = -1e30
FACTOR = HD**-0.5
LOG2E = 1.4426950408889634
SCALE = FACTOR * LOG2E
F32 = jnp.float32
BF16 = jnp.bfloat16


def iota(shape, dim):
    return lax.broadcasted_iota(jnp.int32, shape, dim)


def one_hot(cond):
    return jnp.where(cond, 1.0, 0.0).astype(BF16)


def dot_nt(a, b):
    return lax.dot_general(a, b, (((1,), (1,)), ((), ())), preferred_element_type=F32)


def dot(a, b):
    return jnp.dot(a, b, preferred_element_type=F32)


def kernel(
    act, modul, patch, wt, wo, cache, ids, region, counts,
    out,
    hid, wts, cbuf, keys, vals, pieces, qx, kvx, queries, fresh_k, fresh_v,
    po_send, po, ml_send, ml, gk, woall, part, rs_send, rs_recv, reg, res, place,
    own_sem, hid_ss, hid_rs, q_ss, q_rs, kv_ss, kv_rs, po_ss, po_rs, ml_ss, ml_rs,
    gk_ss, gk_rs, wo_ss, wo_rs, rs_ss, rs_rs, reg_ss, reg_rs, res_ss, res_rs, c_sem, w_sem,
):
    pipe = lax.axis_index("pipe")
    u = lax.axis_index("ulys")
    z, y = u // NY, lax.rem(u, NY)
    rows, width = act.shape
    line = NZ * rows
    half = width // 2
    span = cache.shape[0]
    chunk = span // 3

    def at_y(j):
        return lax.rem(y + j, NY)

    def at_z(k):
        return lax.rem(z + k + NZ, NZ)

    def dev(zz, yy):
        return (pipe, zz * NY + yy)

    after, before = lax.rem(pipe + 1, 8), lax.rem(pipe + 7, 8)

    def remote(src, dst, ss, rs, target):
        return pltpu.make_async_remote_copy(src, dst, ss, rs, target, device_id_type=MESH)

    block = wt.shape[0] // 3
    w_copies = [
        pltpu.make_async_copy(wt.at[pl.ds(i * block, block)], wts.at[pl.ds(i * 128, block)], w_sem.at[i])
        for i in range(3)
    ]
    for copy in w_copies:
        copy.start()

    def cache_copy(i):
        return pltpu.make_async_copy(cache.at[pl.ds(i * 256, 256)], cbuf.at[lax.rem(i, 2)], c_sem.at[lax.rem(i, 2)])

    cache_copy(0).start()

    barrier = pltpu.get_barrier_semaphore()
    greeted = [dev(z, at_y(j)) for j in range(1, NY)] + [dev(at_z(k), y) for k in range(1, NZ)]
    greeted += [(after, u), (before, u)]
    for target in greeted:
        pl.semaphore_signal(barrier, inc=1, device_id=target, device_id_type=MESH)

    lifted = act[...].astype(F32)
    center = jnp.mean(lifted, axis=1, keepdims=True)
    spread = jnp.mean(jnp.square(lifted - center), axis=1, keepdims=True)
    normed = (lifted - center) * lax.rsqrt(spread + 1e-06)
    hid[y, z] = (normed * (1.0 + modul[1]) + modul[0]).astype(BF16)
    diagonal = iota((rows, rows), 0) == iota((rows, rows), 1)
    wide = jnp.broadcast_to(region[...].astype(F32), (rows, rows))
    column = jnp.sum(jnp.where(diagonal, wide, 0.0), axis=1, keepdims=True)
    reg[z] = jnp.broadcast_to(column, (rows, 128))

    slots = ids.shape[0]
    packed = ids[...].reshape(2 * slots, HPD * HD)
    pick = iota((slots, 2 * slots), 1) - 2 * iota((slots, 2 * slots), 0)
    gk[y, :, 0 : HPD * HD] = dot(one_hot(pick == 0), packed).astype(BF16)
    gk[y, :, HPD * HD :] = dot(one_hot(pick == 1), packed).astype(BF16)

    pl.semaphore_wait(barrier, len(greeted))

    sends = []

    def go(copy):
        copy.start()
        sends.append(copy)

    def send_hid(yy, zz, slot, target):
        go(remote(hid.at[yy, zz], hid.at[yy, zz], hid_ss.at[slot], hid_rs.at[yy, zz], target))

    def wait_hid(yy, zz):
        remote(hid.at[yy, zz], hid.at[yy, zz], hid_ss.at[0], hid_rs.at[yy, zz], dev(z, y)).wait_recv()

    slot = iter(range(64))
    up, down = dev(at_z(1), y), dev(at_z(-1), y)
    left, right, far = dev(z, at_y(3)), dev(z, at_y(1)), dev(z, at_y(2))
    for target in (up, down, left, right, far):
        send_hid(y, z, next(slot), target)
    for k in range(1, NZ):
        go(remote(reg.at[z], reg.at[z], reg_ss.at[k - 1], reg_rs.at[z], dev(at_z(k), y)))
    for j in range(1, NY):
        go(remote(gk.at[y], gk.at[y], gk_ss.at[j - 1], gk_rs.at[y], dev(z, at_y(j))))

    spot, goal = iota((NY * 128, HPD * HD), 0), iota((NY * 128, HPD * HD), 1)
    inner = lax.rem(spot, 128)
    found = (spot // 128 == lax.rem(goal, 128) // 32) & (inner // 32 == goal // 128)
    place[...] = one_hot(found & (lax.rem(inner, 32) == lax.rem(goal, 32)))
    for i in range(3):
        wts[pl.ds(i * 128 + block, 128 - block)] = jnp.zeros((128 - block, width), BF16)

    pick_c = iota((256, 512), 1) - 2 * iota((256, 512), 0)
    even, odd = one_hot(pick_c == 0), one_hot(pick_c == 1)

    def split_cache(i, last):
        if not last:
            cache_copy(i + 1).start()
        cache_copy(i).wait()
        x = cbuf[lax.rem(i, 2)].reshape(512, HPD * HD)
        kk = dot(even, x).astype(BF16)
        vv = dot(odd, x).astype(BF16)
        for h in range(HPD):
            keys[h, pl.ds(pl.multiple_of(i * 256, 256), 256)] = kk[:, h * HD : (h + 1) * HD]
            vals[h, pl.ds(pl.multiple_of(i * 256, 256), 256)] = vv[:, h * HD : (h + 1) * HD]

    def split_some(first, count, last=False):
        def body(i, _):
            split_cache(first + i, False)
            return 0

        lax.fori_loop(0, count - (1 if last else 0), body, 0)
        if last:
            split_cache(jnp.int32(first + count - 1), True)

    split_some(0, 4)

    opposite = at_y(2)
    wait_hid(opposite, z)
    send_hid(opposite, z, next(slot), up)
    send_hid(opposite, z, next(slot), down)
    for k in range(1, 5):
        wait_hid(y, at_z(-k))
        if k < 4:
            send_hid(y, at_z(-k), next(slot), up)
        send_hid(y, at_z(-k), next(slot), left)
        send_hid(y, at_z(-k), next(slot), right)
        if k < 4:
            wait_hid(y, at_z(k))
            if k < 3:
                send_hid(y, at_z(k), next(slot), down)
            send_hid(y, at_z(k), next(slot), left)
            send_hid(y, at_z(k), next(slot), right)
        wait_hid(opposite, at_z(k))
        if k < 4:
            send_hid(opposite, at_z(k), next(slot), down)
        if k < 4:
            wait_hid(opposite, at_z(-k))
            if k < 3:
                send_hid(opposite, at_z(-k), next(slot), up)
        split_some(4 + 2 * (k - 1), 2, k == 4)
    for copy in w_copies:
        copy.wait()

    def project(i, _):
        ln = at_y(i)

        @pl.when(lax.rem(i, 2) == 1)
        def _():
            def body(zz, _):
                wait_hid(ln, zz)
                return 0

            lax.fori_loop(0, NZ, body, 0)

        base = pl.multiple_of(ln * line, line)
        x = hid[ln].reshape(line, width)
        pieces[pl.ds(base, line)] = dot_nt(x, wts[...]).astype(BF16)
        qx[y, pl.ds(base, line)] = pieces[pl.ds(base, line), 0:128]

        def send_q(j, _):
            s = pieces.at[pl.ds(base, line), pl.ds(0, 128)]
            d = qx.at[y, pl.ds(base, line)]
            remote(s, d, q_ss.at[j, ln], q_rs.at[y, ln], dev(z, at_y(j))).start()
            return 0

        lax.fori_loop(1, NY, send_q, 0)

        @pl.when(i != 0)
        def _():
            s = pieces.at[pl.ds(base, line), pl.ds(128, 256)]
            remote(s, kvx.at[y], kv_ss.at[i], kv_rs.at[y], dev(z, ln)).start()

        @pl.when(i == 0)
        def _():
            kvx[y] = pieces[pl.ds(base, line), 128:384]

        return 0

    lax.fori_loop(0, NY, project, 0)

    own_wo = pltpu.make_async_copy(wo, woall.at[y], own_sem)
    own_wo.start()
    for j in range(1, NY):
        go(remote(wo, woall.at[y], wo_ss.at[j - 1], wo_rs.at[y], dev(z, at_y(j))))

    def line_ref(ref, ln):
        return ref.at[pl.ds(pl.multiple_of(ln * line, line), line)]

    def recv(ref, rs):
        remote(ref, ref, hid_ss.at[0], rs, dev(z, y)).wait_recv()

    for j in range(1, NY):
        recv(kvx.at[at_y(j)], kv_rs.at[at_y(j)])
    both = [
        sum(dot(kvx[yy, :, s * 128 : s * 128 + 128], place[yy * 128 : yy * 128 + 128]) for yy in range(NY)).astype(BF16)
        for s in range(2)
    ]
    for h in range(HPD):
        fresh_k[h] = both[0][:, h * HD : (h + 1) * HD]
        fresh_v[h] = both[1][:, h * HD : (h + 1) * HD]

    lane = iota((line, 128), 1)

    def attend_head(ln, h, packed_ml):
        q = queries[h, pl.ds(pl.multiple_of(ln * line, line), line)]
        peaks, totals, outs = [], [], []
        for c in range(4):
            if c < 3:
                kk, vv = keys[h, c * chunk : (c + 1) * chunk], vals[h, c * chunk : (c + 1) * chunk]
            else:
                kk, vv = fresh_k[h], fresh_v[h]
            s = dot_nt(q, kk)
            peak = jnp.max(s, axis=1, keepdims=True)
            w = jnp.exp2((s - peak) * SCALE)
            totals.append(jnp.sum(w, axis=1, keepdims=True))
            outs.append(dot(w.astype(BF16), vv))
            if c < 3:
                stale = patch[0] == y * 3 + c
                peak = jnp.where(stale, NEG_BIG, peak)
            peaks.append(peak)
        peak = jnp.maximum(jnp.maximum(peaks[0], peaks[1]), jnp.maximum(peaks[2], peaks[3]))
        alphas = [jnp.exp2((p - peak) * SCALE) for p in peaks]
        total = sum(a * t for a, t in zip(alphas, totals))
        own = sum(a * o for a, o in zip(alphas, outs))
        packed_ml = jnp.where(lane == h, peak, packed_ml)
        packed_ml = jnp.where(lane == h + HPD, total, packed_ml)
        return own / total, packed_ml

    def attend_line(i, _):
        ln = at_y(i + 1)
        base = pl.multiple_of(ln * line, line)
        for j in range(1, NY):
            yy = at_y(j)
            recv(qx.at[yy, pl.ds(base, line)], q_rs.at[yy, ln])
        full = sum(dot(qx[yy, pl.ds(base, line)], place[yy * 128 : yy * 128 + 128]) for yy in range(NY)).astype(BF16)
        for h in range(HPD):
            queries[h, pl.ds(base, line)] = full[:, h * HD : (h + 1) * HD]

        def head(h, packed_ml):
            normal, packed_ml = attend_head(ln, h, packed_ml)
            po_send[ln, h] = normal.astype(BF16)
            return packed_ml

        packed_ml = lax.fori_loop(0, HPD, head, jnp.zeros((line, 128), F32))
        ml_send[ln] = jnp.transpose(packed_ml)[0:8]

        @pl.when(i < NY - 1)
        def _():
            target = dev(z, ln)
            remote(po_send.at[ln], po.at[y], po_ss.at[ln], po_rs.at[y], target).start()
            remote(ml_send.at[ln], ml.at[y], ml_ss.at[ln], ml_rs.at[y], target).start()

        return 0

    lax.fori_loop(0, NY, attend_line, 0)
    po[y] = po_send[y]
    ml[y] = ml_send[y]

    def recv_reg(k, _):
        zz = at_z(k)
        recv(reg.at[zz], reg_rs.at[zz])
        return 0

    lax.fori_loop(1, NZ, recv_reg, 0)
    for j in range(1, NY):
        recv(gk.at[at_y(j)], gk_rs.at[at_y(j)])
    total_slots = NY * slots
    per_subject = slots // SUBJ
    spot = iota((line, total_slots), 1)
    inside = lax.rem(spot, slots)
    subject = inside // per_subject
    slot_index = spot // slots * per_subject + lax.rem(inside, per_subject)
    live = jnp.zeros((line, total_slots), jnp.int32)
    for s in range(SUBJ):
        live = jnp.where(subject == s, counts[0, s], live)
    regions = reg[...].reshape(line, 128)[:, 0:1]
    mask = (regions == (subject + 1).astype(F32)) & (slot_index < live)
    own_base = pl.multiple_of(y * line, line)
    guests = []
    for h in range(HPD):
        q = queries[h, pl.ds(own_base, line)]
        g_keys = gk[:, :, h * HD : (h + 1) * HD].reshape(total_slots, HD)
        g_vals = gk[:, :, (HPD + h) * HD : (HPD + h + 1) * HD].reshape(total_slots, HD)
        s = dot_nt(q, g_keys)
        peak = jnp.max(jnp.where(mask, s, NEG_BIG), axis=1, keepdims=True)
        w = jnp.where(mask, jnp.exp2(jnp.where(mask, (s - peak) * SCALE, 0.0)), 0.0)
        total = jnp.maximum(jnp.sum(w, axis=1, keepdims=True), 1.0)
        guests.append(dot(w.astype(BF16), g_vals) / total)

    for j in range(1, NY):
        recv(po.at[at_y(j)], po_rs.at[at_y(j)])
        recv(ml.at[at_y(j)], ml_rs.at[at_y(j)])
    stats = jnp.concatenate([ml[...].reshape(NY * 8, line), jnp.zeros((128 - NY * 8, line), F32)], axis=0)
    stats = jnp.transpose(stats)
    mixed = []
    for h in range(HPD):
        peaks = [stats[:, yy * 8 + h : yy * 8 + h + 1] for yy in range(NY)]
        totals = [stats[:, yy * 8 + HPD + h : yy * 8 + HPD + h + 1] for yy in range(NY)]
        peak = jnp.maximum(jnp.maximum(peaks[0], peaks[1]), jnp.maximum(peaks[2], peaks[3]))
        shares = [jnp.exp2((p - peak) * SCALE) * t for p, t in zip(peaks, totals)]
        whole = shares[0] + shares[1] + shares[2] + shares[3]
        own = sum(po[yy, h].astype(F32) * (shares[yy] / whole) for yy in range(NY))
        mixed.append((own + guests[h]).astype(BF16))

    own_wo.wait()
    for j in range(1, NY):
        recv(woall.at[at_y(j)], wo_rs.at[at_y(j)])
    spot, goal = iota((HD, NY * block), 0), iota((HD, NY * block), 1)
    ordered = sum(
        dot(
            mixed[h],
            one_hot(
                (lax.rem(goal, block) // 32 == h) & (goal // block == spot // 32) & (lax.rem(goal, 32) == lax.rem(spot, 32))
            ),
        )
        for h in range(HPD)
    ).astype(BF16)
    tile = 512

    def project_out(t, _):
        cols = pl.ds(pl.multiple_of(t * tile, tile), tile)
        w = woall[:, :, cols].reshape(NY * block, tile)
        part[:, :, cols] = dot(ordered, w).reshape(NZ, rows, tile)
        return 0

    lax.fori_loop(0, width // tile, project_out, 0)

    cols = (pl.ds(0, half), pl.ds(half, half))
    for t in range(4):
        for d in range(2):
            for s in range(2):
                hops = 4 if d == s else 3
                if t >= hops:
                    continue
                step = 1 if d == 0 else -1
                term = part[at_z(step * (hops - t)), :, cols[s]]
                if t > 0:
                    recv(rs_recv.at[d, s, t - 1], rs_rs.at[d, s, t - 1])
                    term = term + rs_recv[d, s, t - 1].astype(F32)
                rs_send[d, s, t] = term.astype(BF16)
                go(remote(rs_send.at[d, s, t], rs_recv.at[d, s, t], rs_ss.at[d, s, t], rs_rs.at[d, s, t], dev(at_z(step), y)))
    for s in range(2):
        total = part[z, :, cols[s]]
        for d in range(2):
            last = (4 if d == s else 3) - 1
            recv(rs_recv.at[d, s, last], rs_rs.at[d, s, last])
            total = total + rs_recv[d, s, last].astype(F32)
        gate = modul[2, :, cols[s]]
        res[s] = (act[:, cols[s]].astype(F32) + gate * total).astype(BF16)
        go(remote(res.at[s], out.at[:, cols[s]], res_ss.at[s], res_rs.at[s], (after, u)))
    for s in range(2):
        recv(out.at[:, cols[s]], res_rs.at[s])

    for copy in sends:
        copy.wait_send()

    def drain(i, _):
        ln = at_y(i)
        base = pl.multiple_of(ln * line, line)

        def drain_q(j, _):
            s = pieces.at[pl.ds(base, line), pl.ds(0, 128)]
            remote(s, qx.at[y, pl.ds(base, line)], q_ss.at[j, ln], q_rs.at[y, ln], dev(z, at_y(j))).wait_send()
            return 0

        lax.fori_loop(1, NY, drain_q, 0)

        @pl.when(i != 0)
        def _():
            s = pieces.at[pl.ds(base, line), pl.ds(128, 256)]
            remote(s, kvx.at[y], kv_ss.at[i], kv_rs.at[y], dev(z, ln)).wait_send()
            remote(po_send.at[ln], po.at[y], po_ss.at[ln], po_rs.at[y], dev(z, ln)).wait_send()
            remote(ml_send.at[ln], ml.at[y], ml_ss.at[ln], ml_rs.at[y], dev(z, ln)).wait_send()

        return 0

    lax.fori_loop(0, NY, drain, 0)


def shards(
    activations, patch_index, modulation, qkv_weight, out_weight, stale_cache, id_cache, region_ids, id_counts
):
    _, rows, width = activations.shape
    span = stale_cache.shape[2]
    slots = id_cache.shape[2] * id_cache.shape[3]
    line = NZ * rows
    tokens = NY * line
    block = qkv_weight.shape[2] // 3
    half = width // 2
    dma = pltpu.SemaphoreType.DMA
    vmem = pl.BlockSpec(memory_space=pltpu.VMEM)
    smem = pl.BlockSpec(memory_space=pltpu.SMEM)
    anywhere = pl.BlockSpec(memory_space=pl.ANY)
    result = pl.pallas_call(
        kernel,
        out_shape=jax.ShapeDtypeStruct((rows, width), BF16),
        in_specs=[vmem, vmem, smem, anywhere, anywhere, anywhere, vmem, vmem, smem],
        out_specs=vmem,
        scratch_shapes=[
            pltpu.VMEM((NY, NZ, rows, width), BF16),
            pltpu.VMEM((3 * 128, width), BF16),
            pltpu.VMEM((2, 256, 2, HPD * HD), BF16),
            pltpu.VMEM((HPD, span, HD), BF16),
            pltpu.VMEM((HPD, span, HD), BF16),
            pltpu.VMEM((tokens, 3 * 128), BF16),
            pltpu.VMEM((NY, tokens, 128), BF16),
            pltpu.VMEM((NY, line, 256), BF16),
            pltpu.VMEM((HPD, tokens, HD), BF16),
            pltpu.VMEM((HPD, line, HD), BF16),
            pltpu.VMEM((HPD, line, HD), BF16),
            pltpu.VMEM((NY, HPD, line, HD), BF16),
            pltpu.VMEM((NY, HPD, line, HD), BF16),
            pltpu.VMEM((NY, 8, line), F32),
            pltpu.VMEM((NY, 8, line), F32),
            pltpu.VMEM((NY, slots, 2 * HPD * HD), BF16),
            pltpu.VMEM((NY, block, width), BF16),
            pltpu.VMEM((NZ, rows, width), F32),
            pltpu.VMEM((2, 2, 4, rows, half), BF16),
            pltpu.VMEM((2, 2, 4, rows, half), BF16),
            pltpu.VMEM((NZ, rows, 128), F32),
            pltpu.VMEM((2, rows, half), BF16),
            pltpu.VMEM((NY * 128, HPD * HD), BF16),
            dma,
            dma((64,)), dma((NY, NZ)),
            dma((NY, NY)), dma((NY, NY)),
            dma((NY,)), dma((NY,)),
            dma((NY,)), dma((NY,)),
            dma((NY,)), dma((NY,)),
            dma((NY,)), dma((NY,)),
            dma((NY,)), dma((NY,)),
            dma((2, 2, 4)), dma((2, 2, 4)),
            dma((NZ,)), dma((NZ,)),
            dma((2,)), dma((2,)),
            dma((2,)),
            dma((3,)),
        ],
        compiler_params=pltpu.CompilerParams(
            collective_id=0, has_side_effects=True, vmem_limit_bytes=56 * 2**20
        ),
        name="section",
    )(
        activations[0],
        jnp.transpose(modulation, (1, 0, 2)),
        patch_index,
        jnp.swapaxes(qkv_weight[0], 0, 1),
        out_weight[0],
        stale_cache[0, 0],
        id_cache[0, 0].reshape(slots, 2, HPD * HD),
        region_ids,
        id_counts,
    )
    return result[None]


def solution(mesh):
    placed = (
        P("pipe", "ulys", None),
        P("pipe"),
        P("pipe", None, None),
        P("pipe", None, "ulys"),
        P("pipe", "ulys", None),
        P("pipe", "ulys", None, None, None),
        P("pipe", "ulys", None, None, None, None),
        P("pipe", "ulys"),
        P("pipe", None),
    )
    return jax.shard_map(
        shards, mesh=mesh, in_specs=placed, out_specs=P("pipe", "ulys", None), check_vma=False
    )
```

```python
import functools

import jax
import jax.numpy as jnp
from jax import lax
from jax.experimental import pallas as pl
from jax.experimental.pallas import tpu as pltpu
from jax.sharding import PartitionSpec as P

MESH = pl.DeviceIdType.MESH
HD = 128
HPD = 3
NZ = 8
NY = 4
SUBJ = 6
NEG_BIG = -1e30
FACTOR = HD**-0.5
LOG2E = 1.4426950408889634
SCALE = FACTOR * LOG2E
F32 = jnp.float32
BF16 = jnp.bfloat16


def iota(shape, dim):
    return lax.broadcasted_iota(jnp.int32, shape, dim)


def one_hot(cond):
    return jnp.where(cond, 1.0, 0.0).astype(BF16)


def dot_nt(a, b):
    return lax.dot_general(a, b, (((1,), (1,)), ((), ())), preferred_element_type=F32)


def dot(a, b):
    return jnp.dot(a, b, preferred_element_type=F32)


ORDER = (0, -1, 1, -2, 2, -3, 3, 4)
SLOT = {d: i for i, d in enumerate(ORDER)}
SLOT[-4] = SLOT[4]
GROUPS = ((0, 1), (1, 3), (3, 5), (5, 7), (7, 8))


def kernel(
    act, modul, patch, wt, wo, cache, ids, region, counts,
    out,
    hid, wts, cbuf, keys, vals, pieces, qx, kvx, queries, fresh_k, fresh_v, acc, top, mass,
    po_send, po, ml_send, ml, stats, guest, gk, woall, part, rs_send, rs_recv, res, place, reorder,
    hid_ss, hid_rs, q_ss, q_rs, kv_ss, kv_rs, po_ss, po_rs, ml_ss, ml_rs,
    gk_ss, gk_rs, wo_ss, wo_rs, own_sem, rs_ss, rs_rs, res_ss, res_rs, c_sem, w_sem,
):
    pipe = lax.axis_index("pipe")
    u = lax.axis_index("ulys")
    z, y = u // NY, lax.rem(u, NY)
    rows, width = act.shape
    quad = NY * rows
    line = NZ * rows
    split = (width * 3 // 4) // 128 * 128
    span = cache.shape[0]
    chunk = span // 3

    def at_y(j):
        return lax.rem(y + j, NY)

    def at_z(k):
        return lax.rem(z + k + NZ, NZ)

    def dev(zz, yy):
        return (pipe, zz * NY + yy)

    after, before = lax.rem(pipe + 1, 8), lax.rem(pipe + 7, 8)
    up, down = dev(at_z(1), y), dev(at_z(-1), y)
    right, far, left = (dev(z, at_y(j)) for j in range(1, NY))
    peers = (right, far, left)

    def remote(src, dst, ss, rs, target):
        return pltpu.make_async_remote_copy(src, dst, ss, rs, target, device_id_type=MESH)

    block = wt.shape[0] // 3
    w_copies = [
        pltpu.make_async_copy(wt.at[pl.ds(i * block, block)], wts.at[pl.ds(i * 128, block)], w_sem.at[i])
        for i in range(3)
    ]
    for copy in w_copies:
        copy.start()

    def cache_copy(i):
        return pltpu.make_async_copy(cache.at[pl.ds(i * 256, 256)], cbuf.at[lax.rem(i, 2)], c_sem.at[lax.rem(i, 2)])

    cache_copy(0).start()
    own_wo = pltpu.make_async_copy(wo, woall.at[y], own_sem)
    own_wo.start()

    barrier = pltpu.get_barrier_semaphore()
    greeted = [right, far, left, up, down, (after, u), (before, u)]
    for target in greeted:
        pl.semaphore_signal(barrier, inc=1, device_id=target, device_id_type=MESH)

    lifted = act[...].astype(F32)
    center = jnp.mean(lifted, axis=1, keepdims=True)
    spread = jnp.mean(jnp.square(lifted - center), axis=1, keepdims=True)
    normed = (lifted - center) * lax.rsqrt(spread + 1e-06)
    hid[0, y, :, 0:width] = (normed * (1.0 + modul[1]) + modul[0]).astype(BF16)
    diagonal = iota((rows, rows), 0) == iota((rows, rows), 1)
    wide = jnp.broadcast_to(region[...].astype(F32), (rows, rows))
    column = jnp.sum(jnp.where(diagonal, wide, 0.0), axis=1, keepdims=True)
    hid[0, y, :, width:] = jnp.broadcast_to(column, (rows, 128)).astype(BF16)

    slots = ids.shape[0]
    packed = ids[...].reshape(2 * slots, HPD * HD)
    pick = iota((slots, 2 * slots), 1) - 2 * iota((slots, 2 * slots), 0)
    gk[y, :, 0 : HPD * HD] = dot(one_hot(pick == 0), packed).astype(BF16)
    gk[y, :, HPD * HD :] = dot(one_hot(pick == 1), packed).astype(BF16)

    pl.semaphore_wait(barrier, len(greeted))

    sends = []

    def go(copy):
        copy.start()
        sends.append(copy)

    def recv(ref, rs):
        remote(ref, ref, hid_ss.at[0], rs, dev(z, y)).wait_recv()

    parts = {
        "r": (pl.ds(0, width + 128), 0),
        "w": (pl.ds(0, width), 0),
        "a": (pl.ds(0, split), 0),
        "b": (pl.ds(width - split, split), 0),
        "c": (pl.ds(0, width - split), 1),
        "d": (pl.ds(split, width - split), 1),
    }
    next_send = iter(range(64))

    def send_hid(d, yy, what, target, d_there):
        cols, n = parts[what]
        src, dst = hid.at[SLOT[d], yy, :, cols], hid.at[SLOT[d_there], yy, :, cols]
        go(remote(src, dst, hid_ss.at[next(next_send)], hid_rs.at[SLOT[d_there], yy, n], target))

    def wait_hid(d, yy, what):
        cols, n = parts[what]
        recv(hid.at[SLOT[d], yy, :, cols], hid_rs.at[SLOT[d], yy, n])

    streams = ((y, "r", 4, 3), (at_y(1), "a", 4, 3), (at_y(3), "b", 3, 4), (at_y(2), "w", 3, 4))

    wo_half = [pl.ds(i * (block // 2), block // 2) for i in range(2)]

    def wait_wo(yy, i):
        recv(woall.at[yy, wo_half[i]], wo_rs.at[yy, i])

    def send_wo(i):
        for j, target in enumerate((right, left)):
            go(remote(wo.at[wo_half[i]], woall.at[y, wo_half[i]], wo_ss.at[j, i], wo_rs.at[y, i], target))

    def pass_wo():
        for i, (yy, target) in enumerate(((at_y(3), right), (at_y(1), left))):
            wait_wo(yy, i)
            ref = woall.at[yy, wo_half[i]]
            go(remote(ref, ref, wo_ss.at[2, i], wo_rs.at[yy, i], target))

    send_hid(0, y, "r", up, -1)
    send_hid(0, y, "r", down, 1)
    for what, target in (("a", left), ("b", right), ("w", far), ("d", left), ("c", right)):
        send_hid(0, y, what, target, 0)

    spot, goal = iota((NY * 128, HPD * HD), 0), iota((NY * 128, HPD * HD), 1)
    inner = lax.rem(spot, 128)
    found = (spot // 128 == lax.rem(goal, 128) // 32) & (inner // 32 == goal // 128)
    place[...] = one_hot(found & (lax.rem(inner, 32) == lax.rem(goal, 32)))
    spot, goal = iota((HPD * HD, NY * block), 0), iota((HPD * HD, NY * block), 1)
    found = (goal // block == lax.rem(spot, HD) // 32) & (lax.rem(goal, block) // 32 == spot // HD)
    reorder[...] = one_hot(found & (lax.rem(goal, 32) == lax.rem(spot, 32)))
    for i in range(3):
        wts[pl.ds(i * 128 + block, 128 - block)] = jnp.zeros((128 - block, width), BF16)

    pick_c = iota((256, 512), 1) - 2 * iota((256, 512), 0)
    even, odd = one_hot(pick_c == 0), one_hot(pick_c == 1)

    def split_cache(i, last):
        if not last:
            cache_copy(i + 1).start()
        cache_copy(i).wait()
        x = cbuf[lax.rem(i, 2)].reshape(512, HPD * HD)
        kk = dot(even, x).astype(BF16)
        vv = dot(odd, x).astype(BF16)
        for h in range(HPD):
            keys[h, pl.ds(pl.multiple_of(i * 256, 256), 256)] = kk[:, h * HD : (h + 1) * HD]
            vals[h, pl.ds(pl.multiple_of(i * 256, 256), 256)] = vv[:, h * HD : (h + 1) * HD]

    def split_some(first, count, last=False):
        def body(i, _):
            split_cache(first + i, False)
            return 0

        lax.fori_loop(0, count - (1 if last else 0), body, 0)
        if last:
            split_cache(jnp.int32(first + count - 1), True)

    def span_of(g):
        first, end = GROUPS[g]
        return first * quad, (end - first) * quad

    def project(g):
        first, end = GROUPS[g]
        for d in ORDER[first:end]:
            wait_hid(d, at_y(3), "c")
            wait_hid(d, at_y(1), "d")
        base, size = span_of(g)
        x = hid[first:end, :, :, 0:width].reshape(size, width)
        p = dot_nt(x, wts[...]).astype(BF16)
        pieces[first:end] = p.reshape(end - first, NY, rows, 3 * 128)
        qx[y, pl.ds(base, size)] = p[:, 0:128]
        for j, target in enumerate(peers):
            q = qx.at[y, pl.ds(base, size)]
            go(remote(q, q, q_ss.at[g, j], q_rs.at[g, y], target))
        for j, target in enumerate(peers):
            kv = pieces.at[pl.ds(first, end - first), at_y(j + 1), :, pl.ds(128, 256)]
            go(remote(kv, kvx.at[y, pl.ds(first, end - first)], kv_ss.at[g, j], kv_rs.at[g, y], target))
        kvx[y, first:end] = pieces[first:end, y, :, 128:384]

    lane = iota((256, 128), 1)

    def place_queries(g):
        base, size = span_of(g)
        for j in range(1, NY):
            recv(qx.at[at_y(j), pl.ds(base, size)], q_rs.at[g, at_y(j)])
        full = sum(dot(qx[yy, pl.ds(base, size)], place[yy * 128 : yy * 128 + 128]) for yy in range(NY)).astype(BF16)
        for h in range(HPD):
            queries[h, pl.ds(base, size)] = full[:, h * HD : (h + 1) * HD]

    def attend_keys(h, base, size, with_fresh):
        q = queries[h, pl.ds(base, size)]
        scores = [dot_nt(q, keys[h, c * chunk : (c + 1) * chunk]) for c in range(3)]
        peaks = [jnp.max(s, axis=1, keepdims=True) for s in scores]
        replaced = [patch[0] == y * 3 + c for c in range(3)]
        peaks = [jnp.where(r, NEG_BIG, p) for r, p in zip(replaced, peaks)]
        peak = jnp.maximum(jnp.maximum(peaks[0], peaks[1]), peaks[2])
        if with_fresh:
            fresh_scores = dot_nt(q, fresh_k[h])
            peak = jnp.maximum(peak, jnp.max(fresh_scores, axis=1, keepdims=True))
        total, own = 0.0, 0.0
        for c in range(3):
            w = jnp.exp2((scores[c] - jnp.where(replaced[c], -NEG_BIG, peak)) * SCALE)
            total = total + jnp.sum(w, axis=1, keepdims=True)
            own = own + dot(w.astype(BF16), vals[h, c * chunk : (c + 1) * chunk])
        if with_fresh:
            w = jnp.exp2((fresh_scores - peak) * SCALE)
            total = total + jnp.sum(w, axis=1, keepdims=True)
            own = own + dot(w.astype(BF16), fresh_v[h])
        return peak, total, own

    def attend(g):
        base, size = span_of(g)
        place_queries(g)

        def head(h, _):
            peak, total, own = attend_keys(h, base, size, False)
            acc[h, pl.ds(base, size)] = own
            top[h, pl.ds(base, size)] = jnp.broadcast_to(peak, (size, 128))
            mass[h, pl.ds(base, size)] = jnp.broadcast_to(total, (size, 128))
            return 0

        lax.fori_loop(0, HPD, head, 0)

    total_slots = NY * slots
    per_subject = slots // SUBJ

    def attend_guests(g):
        first, end = GROUPS[g]
        mine = (end - first) * rows
        spot = iota((mine, total_slots), 1)
        inside = lax.rem(spot, slots)
        subject = inside // per_subject
        slot_index = spot // slots * per_subject + lax.rem(inside, per_subject)
        live = jnp.zeros((mine, total_slots), jnp.int32)
        for s in range(SUBJ):
            live = jnp.where(subject == s, counts[0, s], live)
        regions = hid[first:end, y, :, width:].reshape(mine, 128).astype(F32)[:, 0:1]
        mask = (regions == (subject + 1).astype(F32)) & (slot_index < live)
        for h in range(HPD):
            own_rows = [queries[h, pl.ds(pl.multiple_of(i * quad + y * rows, rows), rows)] for i in range(first, end)]
            q = jnp.concatenate(own_rows, axis=0)
            g_keys = gk[:, :, h * HD : (h + 1) * HD].reshape(total_slots, HD)
            g_vals = gk[:, :, (HPD + h) * HD : (HPD + h + 1) * HD].reshape(total_slots, HD)
            s = dot_nt(q, g_keys)
            peak = jnp.max(jnp.where(mask, s, NEG_BIG), axis=1, keepdims=True)
            w = jnp.where(mask, jnp.exp2(jnp.where(mask, (s - peak) * SCALE, 0.0)), 0.0)
            total = jnp.maximum(jnp.sum(w, axis=1, keepdims=True), 1.0)
            guest[h, first * rows : end * rows] = dot(w.astype(BF16), g_vals) / total

    def send_group(g, packed_ml):
        first, end = GROUPS[g]
        base, size = span_of(g)
        for j, target in enumerate(peers):
            src = po_send.at[pl.ds(first, end - first), at_y(j + 1)]
            go(remote(src, po.at[y, pl.ds(first, end - first)], po_ss.at[g, j], po_rs.at[g, y], target))
        ml_send[:, base : base + size] = jnp.transpose(packed_ml)[0:8]
        for j, target in enumerate(peers):
            src, dst = ml_send.at[:, pl.ds(base, size)], ml.at[y, :, pl.ds(base, size)]
            go(remote(src, dst, ml_ss.at[g, j], ml_rs.at[g, y], target))
        po[y, first:end] = po_send[first:end, y]
        ml[y, :, base : base + size] = ml_send[:, base : base + size]

    def pack_ml(packed_ml, h, peak, total, size):
        packed_ml = jnp.where(lane[0:size] == h, peak, packed_ml)
        return jnp.where(lane[0:size] == h + HPD, total, packed_ml)

    def attend_last(g):
        first, end = GROUPS[g]
        base, size = span_of(g)

        def head(h, packed_ml):
            peak, total, own = attend_keys(h, base, size, True)
            acc[h, pl.ds(base, size)] = own / total
            return pack_ml(packed_ml, h, peak, total, size)

        packed_ml = lax.fori_loop(0, HPD, head, jnp.zeros((size, 128), F32))
        for h in range(HPD):
            normal = acc[h, pl.ds(base, size)].astype(BF16)
            po_send[first:end, :, :, h * HD : (h + 1) * HD] = normal.reshape(end - first, NY, rows, HD)
        send_group(g, packed_ml)

    def finish_group(g):
        first, end = GROUPS[g]
        base, size = span_of(g)
        packed_ml = jnp.zeros((size, 128), F32)
        for h in range(HPD):
            s = dot_nt(queries[h, pl.ds(base, size)], fresh_k[h])
            old_peak = top[h, pl.ds(base, size)]
            peak = jnp.maximum(jnp.max(s, axis=1, keepdims=True), old_peak)
            w = jnp.exp2((s - jnp.concatenate([peak, peak], axis=1)) * SCALE)
            alpha = jnp.exp2((old_peak - peak) * SCALE)
            total = jnp.sum(w, axis=1, keepdims=True) + alpha * mass[h, pl.ds(base, size)]
            own = (dot(w.astype(BF16), fresh_v[h]) + alpha * acc[h, pl.ds(base, size)]) / total
            po_send[first:end, :, :, h * HD : (h + 1) * HD] = own.astype(BF16).reshape(end - first, NY, rows, HD)
            packed_ml = pack_ml(packed_ml, h, peak, total, size)
        send_group(g, packed_ml)

    def merge(g):
        first, end = GROUPS[g]
        base, size = span_of(g)
        mine = (end - first) * rows
        for j in range(1, NY):
            recv(ml.at[at_y(j), :, pl.ds(base, size)], ml_rs.at[g, at_y(j)])
            recv(po.at[at_y(j), pl.ds(first, end - first)], po_rs.at[g, at_y(j)])
        packed = jnp.concatenate([ml[yy, :, base : base + size] for yy in range(NY)] + [jnp.zeros((128 - NY * 8, size), F32)], axis=0)
        stats[first:end] = jnp.transpose(packed).reshape(end - first, NY, rows, 128)
        stat = stats[first:end, y].reshape(mine, 128)
        mixed = []
        for h in range(HPD):
            peaks = [stat[:, yy * 8 + h : yy * 8 + h + 1] for yy in range(NY)]
            totals = [stat[:, yy * 8 + HPD + h : yy * 8 + HPD + h + 1] for yy in range(NY)]
            peak = jnp.maximum(jnp.maximum(peaks[0], peaks[1]), jnp.maximum(peaks[2], peaks[3]))
            shares = [jnp.exp2((p - peak) * SCALE) * t for p, t in zip(peaks, totals)]
            whole = shares[0] + shares[1] + shares[2] + shares[3]
            own = sum(
                po[yy, first:end, :, h * HD : (h + 1) * HD].reshape(mine, HD).astype(F32) * (shares[yy] / whole)
                for yy in range(NY)
            )
            mixed.append((own + guest[h, first * rows : end * rows]).astype(BF16))
        ordered = dot(jnp.concatenate(mixed, axis=1), reorder[...]).astype(BF16)
        tile = 512

        def project_out(t, _):
            cols = pl.ds(pl.multiple_of(t * tile, tile), tile)
            w = woall[:, :, cols].reshape(NY * block, tile)
            part[first:end, :, cols] = dot(ordered, w).reshape(end - first, rows, tile)
            return 0

        lax.fori_loop(0, width // tile, project_out, 0)

    for yy, what, _, _ in streams[1:]:
        wait_hid(0, yy, what)
        send_hid(0, yy, what, up, -1)
        send_hid(0, yy, what, down, 1)
    for j, target in enumerate(peers):
        go(remote(gk.at[y], gk.at[y], gk_ss.at[j], gk_rs.at[y], target))
    send_wo(0)
    split_some(0, 6)
    for copy in w_copies:
        copy.wait()
    project(0)
    for k in range(1, 5):
        for yy, what, hops_up, hops_down in streams:
            for sign, hops, onward in ((-1, hops_up, up), (1, hops_down, down)):
                if k > hops:
                    continue
                d = sign * k
                wait_hid(d, yy, what)
                if k < hops:
                    send_hid(d, yy, what, onward, d + sign)
                if what == "r":
                    send_hid(d, yy, "c", right, d)
                    send_hid(d, yy, "d", left, d)
                if k == 4 and what == "r":
                    attend(3)
                    attend_guests(3)
        if k == 1:
            send_wo(1)
        if k == 2:
            pass_wo()
        if k == 1:
            split_some(6, 6, True)
            project(1)
            attend(0)
        if k == 2:
            project(2)
            attend(1)
            attend(2)
        if k == 3:
            project(3)
            for j in range(1, NY):
                recv(gk.at[at_y(j)], gk_rs.at[at_y(j)])
            for g in range(3):
                attend_guests(g)
    project(4)

    for g in range(5):
        first, end = GROUPS[g]
        for j in range(1, NY):
            recv(kvx.at[at_y(j), pl.ds(first, end - first)], kv_rs.at[g, at_y(j)])
    for s, fresh in enumerate((fresh_k, fresh_v)):
        both = sum(
            dot(kvx[yy, :, :, s * 128 : s * 128 + 128].reshape(line, 128), place[yy * 128 : yy * 128 + 128])
            for yy in range(NY)
        ).astype(BF16)
        for h in range(HPD):
            fresh[h] = both[:, h * HD : (h + 1) * HD]
    place_queries(4)
    attend_last(4)
    finish_group(3)
    attend_guests(4)
    own_wo.wait()
    for j, i in ((1, 0), (2, 0), (2, 1), (3, 1)):
        wait_wo(at_y(j), i)

    wide_tile = width // 4
    cols = [pl.ds(i * wide_tile, wide_tile) for i in range(4)]
    order = ((0, 0), (1, 1), (0, 2), (1, 3), (0, 1), (1, 0), (0, 3), (1, 2))
    for dist in (4, 3, 2, 1):
        merge(dist)
        for d, s in order:
            hops = 4 if d == s % 2 else 3
            if dist > hops:
                continue
            step = 1 if d == 0 else -1
            term = part[SLOT[step * dist], :, cols[s]]
            if dist < hops:
                recv(rs_recv.at[d, s, dist], rs_rs.at[d, s, dist])
                term = term + rs_recv[d, s, dist].astype(F32)
            rs_send[d, s, dist - 1] = term.astype(BF16)
            target = up if d == 0 else down
            n = dist - 1
            go(remote(rs_send.at[d, s, n], rs_recv.at[d, s, n], rs_ss.at[d, s, n], rs_rs.at[d, s, n], target))
        if dist > 1:
            finish_group(dist - 2)
    merge(0)
    for s in (0, 2, 1, 3):
        total = part[0, :, cols[s]]
        for d in range(2):
            recv(rs_recv.at[d, s, 0], rs_rs.at[d, s, 0])
            total = total + rs_recv[d, s, 0].astype(F32)
        gate = modul[2, :, cols[s]]
        res[s] = (act[:, cols[s]].astype(F32) + gate * total).astype(BF16)
        go(remote(res.at[s], out.at[:, cols[s]], res_ss.at[s], res_rs.at[s], (after, u)))
    for s in range(4):
        recv(out.at[:, cols[s]], res_rs.at[s])
    for copy in sends:
        copy.wait_send()


def shards(
    activations, patch_index, modulation, qkv_weight, out_weight, stale_cache, id_cache, region_ids, id_counts
):
    _, rows, width = activations.shape
    span = stale_cache.shape[2]
    slots = id_cache.shape[2] * id_cache.shape[3]
    line = NZ * rows
    tokens = NY * line
    block = qkv_weight.shape[2] // 3
    dma = pltpu.SemaphoreType.DMA
    vmem = pl.BlockSpec(memory_space=pltpu.VMEM)
    smem = pl.BlockSpec(memory_space=pltpu.SMEM)
    anywhere = pl.BlockSpec(memory_space=pl.ANY)
    result = pl.pallas_call(
        kernel,
        out_shape=jax.ShapeDtypeStruct((rows, width), BF16),
        in_specs=[vmem, vmem, smem, anywhere, anywhere, anywhere, vmem, vmem, smem],
        out_specs=vmem,
        scratch_shapes=[
            pltpu.VMEM((NZ, NY, rows, width + 128), BF16),
            pltpu.VMEM((3 * 128, width), BF16),
            pltpu.VMEM((2, 256, 2, HPD * HD), BF16),
            pltpu.VMEM((HPD, span, HD), BF16),
            pltpu.VMEM((HPD, span, HD), BF16),
            pltpu.VMEM((NZ, NY, rows, 3 * 128), BF16),
            pltpu.VMEM((NY, tokens, 128), BF16),
            pltpu.VMEM((NY, NZ, rows, 256), BF16),
            pltpu.VMEM((HPD, tokens, HD), BF16),
            pltpu.VMEM((HPD, line, HD), BF16),
            pltpu.VMEM((HPD, line, HD), BF16),
            pltpu.VMEM((HPD, tokens, HD), F32),
            pltpu.VMEM((HPD, tokens, 128), F32),
            pltpu.VMEM((HPD, tokens, 128), F32),
            pltpu.VMEM((NZ, NY, rows, HPD * HD), BF16),
            pltpu.VMEM((NY, NZ, rows, HPD * HD), BF16),
            pltpu.VMEM((8, tokens), F32),
            pltpu.VMEM((NY, 8, tokens), F32),
            pltpu.VMEM((NZ, NY, rows, 128), F32),
            pltpu.VMEM((HPD, line, HD), F32),
            pltpu.VMEM((NY, slots, 2 * HPD * HD), BF16),
            pltpu.VMEM((NY, block, width), BF16),
            pltpu.VMEM((NZ, rows, width), F32),
            pltpu.VMEM((2, 4, 4, rows, width // 4), BF16),
            pltpu.VMEM((2, 4, 4, rows, width // 4), BF16),
            pltpu.VMEM((4, rows, width // 4), BF16),
            pltpu.VMEM((NY * 128, HPD * HD), BF16),
            pltpu.VMEM((HPD * HD, NY * block), BF16),
            dma((64,)), dma((NZ, NY, 2)),
            dma((5, 3)), dma((5, NY)),
            dma((5, 3)), dma((5, NY)),
            dma((5, 3)), dma((5, NY)),
            dma((5, 3)), dma((5, NY)),
            dma((3,)), dma((NY,)),
            dma((3, 2)), dma((NY, 2)),
            dma,
            dma((2, 4, 4)), dma((2, 4, 4)),
            dma((4,)), dma((4,)),
            dma((2,)),
            dma((3,)),
        ],
        compiler_params=pltpu.CompilerParams(
            collective_id=0, has_side_effects=True, vmem_limit_bytes=56 * 2**20
        ),
        name="section",
    )(
        activations[0],
        jnp.transpose(modulation, (1, 0, 2)),
        patch_index,
        jnp.swapaxes(qkv_weight[0], 0, 1),
        out_weight[0],
        stale_cache[0, 0],
        id_cache[0, 0].reshape(slots, 2, HPD * HD),
        region_ids,
        id_counts,
    )
    return result[None]


def solution(mesh):
    placed = (
        P("pipe", "ulys", None),
        P("pipe"),
        P("pipe", None, None),
        P("pipe", None, "ulys"),
        P("pipe", "ulys", None),
        P("pipe", "ulys", None, None, None),
        P("pipe", "ulys", None, None, None, None),
        P("pipe", "ulys"),
        P("pipe", None),
    )
    return jax.shard_map(
        shards, mesh=mesh, in_specs=placed, out_specs=P("pipe", "ulys", None), check_vma=False
    )
```

```python
import functools

import jax
import jax.numpy as jnp
from jax import lax
from jax.experimental import pallas as pl
from jax.experimental.pallas import tpu as pltpu
from jax.sharding import PartitionSpec as P

MESH = pl.DeviceIdType.MESH
HD = 128
HPD = 3
NZ = 8
NY = 4
SUBJ = 6
NEG_BIG = -1e30
FACTOR = HD**-0.5
LOG2E = 1.4426950408889634
SCALE = FACTOR * LOG2E
F32 = jnp.float32
BF16 = jnp.bfloat16


def iota(shape, dim):
    return lax.broadcasted_iota(jnp.int32, shape, dim)


def one_hot(cond):
    return jnp.where(cond, 1.0, 0.0).astype(BF16)


def dot_nt(a, b):
    return lax.dot_general(a, b, (((1,), (1,)), ((), ())), preferred_element_type=F32)


def dot(a, b):
    return jnp.dot(a, b, preferred_element_type=F32)


ORDER = (0, -1, 1, -2, 2, -3, 3, 4)
SLOT = {d: i for i, d in enumerate(ORDER)}
SLOT[-4] = SLOT[4]
NEAR = 2
GROUPS = ((0, 1), (1, 3), (3, 5), (5, 7), (7, 8))


def kernel(
    act, modul, patch, wt, wo, cache, ids, region, counts,
    out,
    hid, wts, cbuf, keys, vals, pieces, qx, kvx, queries, fresh_k, fresh_v, acc, top, mass,
    po_send, po, guest, gk, woall, part, rs_send, rs_recv, res, place, reorder,
    hid_ss, hid_rs, q_ss, q_rs, kv_ss, kv_rs, po_ss, po_rs,
    gk_ss, gk_rs, wo_ss, wo_rs, own_sem, rs_ss, rs_rs, res_ss, res_rs, c_sem, w_sem,
):
    pipe = lax.axis_index("pipe")
    u = lax.axis_index("ulys")
    z, y = u // NY, lax.rem(u, NY)
    rows, width = act.shape
    quad = NY * rows
    line = NZ * rows
    split = width // 2
    span = cache.shape[0]
    chunk = span // 3

    def at_y(j):
        return lax.rem(y + j, NY)

    def at_z(k):
        return lax.rem(z + k + NZ, NZ)

    def dev(zz, yy):
        return (pipe, zz * NY + yy)

    after, before = lax.rem(pipe + 1, 8), lax.rem(pipe + 7, 8)
    up, down = dev(at_z(1), y), dev(at_z(-1), y)
    right, far, left = (dev(z, at_y(j)) for j in range(1, NY))
    peers = (right, far, left)

    def remote(src, dst, ss, rs, target):
        return pltpu.make_async_remote_copy(src, dst, ss, rs, target, device_id_type=MESH)

    block = wt.shape[0] // 3
    w_copies = [
        pltpu.make_async_copy(wt.at[pl.ds(i * block, block)], wts.at[pl.ds(i * 128, block)], w_sem.at[i])
        for i in range(3)
    ]
    for copy in w_copies:
        copy.start()

    def cache_copy(i):
        return pltpu.make_async_copy(cache.at[pl.ds(i * 256, 256)], cbuf.at[lax.rem(i, 2)], c_sem.at[lax.rem(i, 2)])

    cache_copy(0).start()
    own_wo = pltpu.make_async_copy(wo, woall.at[y], own_sem)
    own_wo.start()

    barrier = pltpu.get_barrier_semaphore()
    greeted = [right, far, left, up, down, (after, u), (before, u)]
    for target in greeted:
        pl.semaphore_signal(barrier, inc=1, device_id=target, device_id_type=MESH)

    lifted = act[...].astype(F32)
    center = jnp.mean(lifted, axis=1, keepdims=True)
    spread = jnp.mean(jnp.square(lifted - center), axis=1, keepdims=True)
    normed = (lifted - center) * lax.rsqrt(spread + 1e-06)
    hid[0, y, :, 0:width] = (normed * (1.0 + modul[1]) + modul[0]).astype(BF16)
    diagonal = iota((rows, rows), 0) == iota((rows, rows), 1)
    wide = jnp.broadcast_to(region[...].astype(F32), (rows, rows))
    column = jnp.sum(jnp.where(diagonal, wide, 0.0), axis=1, keepdims=True)
    hid[0, y, :, width:] = jnp.broadcast_to(column, (rows, 128)).astype(BF16)

    slots = ids.shape[0]
    packed = ids[...].reshape(2 * slots, HPD * HD)
    pick = iota((slots, 2 * slots), 1) - 2 * iota((slots, 2 * slots), 0)
    gk[y, :, 0 : HPD * HD] = dot(one_hot(pick == 0), packed).astype(BF16)
    gk[y, :, HPD * HD :] = dot(one_hot(pick == 1), packed).astype(BF16)

    pl.semaphore_wait(barrier, len(greeted))

    sends = []

    def go(copy):
        copy.start()
        sends.append(copy)

    def drain(keep=0):
        done = sends[: len(sends) - keep]
        del sends[: len(sends) - keep]
        for copy in done:
            copy.wait_send()

    def recv(ref, rs):
        remote(ref, ref, hid_ss.at[0], rs, dev(z, y)).wait_recv()

    parts = {
        "r": (pl.ds(0, width + 128), 0),
        "w": (pl.ds(0, width), 0),
        "a": (pl.ds(0, split), 0),
        "b": (pl.ds(width - split, split), 0),
        "c": (pl.ds(0, width - split), 1),
        "d": (pl.ds(split, width - split), 1),
    }
    next_send = iter(range(64))

    def send_hid(d, yy, what, target, d_there):
        cols, n = parts[what]
        src, dst = hid.at[SLOT[d], yy, :, cols], hid.at[SLOT[d_there], yy, :, cols]
        go(remote(src, dst, hid_ss.at[next(next_send)], hid_rs.at[SLOT[d_there], yy, n], target))

    def wait_hid(d, yy, what):
        cols, n = parts[what]
        recv(hid.at[SLOT[d], yy, :, cols], hid_rs.at[SLOT[d], yy, n])

    streams = ((y, "r", 4, 3), (at_y(2), "w", 3, 4), (at_y(1), "a", 4, 3), (at_y(3), "b", 3, 4))
    lateral = {"a": "d", "b": "c"}

    def part_at(what, k):
        return "w" if what in lateral and k > NEAR else what

    wo_half = [pl.ds(i * (block // 2), block // 2) for i in range(2)]

    def wait_wo(yy, i):
        recv(woall.at[yy, wo_half[i]], wo_rs.at[yy, i])

    def send_wo(i):
        for j, target in enumerate((right, left)):
            go(remote(wo.at[wo_half[i]], woall.at[y, wo_half[i]], wo_ss.at[j, i], wo_rs.at[y, i], target))

    def pass_wo():
        for i, (yy, target) in enumerate(((at_y(3), right), (at_y(1), left))):
            wait_wo(yy, i)
            ref = woall.at[yy, wo_half[i]]
            go(remote(ref, ref, wo_ss.at[2, i], wo_rs.at[yy, i], target))

    send_hid(0, y, "r", up, -1)
    send_hid(0, y, "r", down, 1)
    for what, target in (("a", left), ("b", right), ("w", far), ("d", left), ("c", right)):
        send_hid(0, y, what, target, 0)

    spot, goal = iota((NY * 128, HPD * HD), 0), iota((NY * 128, HPD * HD), 1)
    inner = lax.rem(spot, 128)
    found = (spot // 128 == lax.rem(goal, 128) // 32) & (inner // 32 == goal // 128)
    place[...] = one_hot(found & (lax.rem(inner, 32) == lax.rem(goal, 32)))
    spot, goal = iota((HPD * HD, NY * block), 0), iota((HPD * HD, NY * block), 1)
    found = (goal // block == lax.rem(spot, HD) // 32) & (lax.rem(goal, block) // 32 == spot // HD)
    reorder[...] = one_hot(found & (lax.rem(goal, 32) == lax.rem(spot, 32)))
    for i in range(3):
        wts[pl.ds(i * 128 + block, 128 - block)] = jnp.zeros((128 - block, width), BF16)

    pick_c = iota((256, 512), 1) - 2 * iota((256, 512), 0)
    even, odd = one_hot(pick_c == 0), one_hot(pick_c == 1)

    def split_cache(i, last):
        if not last:
            cache_copy(i + 1).start()
        cache_copy(i).wait()
        x = cbuf[lax.rem(i, 2)].reshape(512, HPD * HD)
        kk = dot(even, x).astype(BF16)
        vv = dot(odd, x).astype(BF16)
        for h in range(HPD):
            keys[h, pl.ds(pl.multiple_of(i * 256, 256), 256)] = kk[:, h * HD : (h + 1) * HD]
            vals[h, pl.ds(pl.multiple_of(i * 256, 256), 256)] = vv[:, h * HD : (h + 1) * HD]

    def split_some(first, count, last=False):
        def body(i, _):
            split_cache(first + i, False)
            return 0

        lax.fori_loop(0, count - (1 if last else 0), body, 0)
        if last:
            split_cache(jnp.int32(first + count - 1), True)

    def span_of(g):
        first, end = GROUPS[g]
        return first * quad, (end - first) * quad

    def project(g):
        first, end = GROUPS[g]
        for d in ORDER[first:end]:
            if abs(d) < NEAR:
                wait_hid(d, at_y(3), "c")
                wait_hid(d, at_y(1), "d")
        base, size = span_of(g)
        x = hid[first:end, :, :, 0:width].reshape(size, width)
        p = dot_nt(x, wts[...]).astype(BF16)
        pieces[first:end] = p.reshape(end - first, NY, rows, 3 * 128)
        qx[y, pl.ds(base, size)] = p[:, 0:128]
        for j, target in enumerate(peers):
            q = qx.at[y, pl.ds(base, size)]
            go(remote(q, q, q_ss.at[g, j], q_rs.at[g, y], target))
        for j, target in enumerate(peers):
            kv = pieces.at[pl.ds(first, end - first), at_y(j + 1), :, pl.ds(128, 256)]
            go(remote(kv, kvx.at[y, pl.ds(first, end - first)], kv_ss.at[g, j], kv_rs.at[g, y], target))
        kvx[y, first:end] = pieces[first:end, y, :, 128:384]

    lane = iota((256, 128), 1)

    def place_queries(g):
        base, size = span_of(g)
        for j in range(1, NY):
            recv(qx.at[at_y(j), pl.ds(base, size)], q_rs.at[g, at_y(j)])
        full = sum(dot(qx[yy, pl.ds(base, size)], place[yy * 128 : yy * 128 + 128]) for yy in range(NY)).astype(BF16)
        for h in range(HPD):
            queries[h, pl.ds(base, size)] = full[:, h * HD : (h + 1) * HD]

    def place_fresh(g_first, g_end):
        for g in range(g_first, g_end):
            first, end = GROUPS[g]
            for j in range(1, NY):
                recv(kvx.at[at_y(j), pl.ds(first, end - first)], kv_rs.at[g, at_y(j)])
        first, end = GROUPS[g_first][0], GROUPS[g_end - 1][1]
        size = (end - first) * rows
        for s, fresh in enumerate((fresh_k, fresh_v)):
            both = sum(
                dot(kvx[yy, first:end, :, s * 128 : s * 128 + 128].reshape(size, 128), place[yy * 128 : yy * 128 + 128])
                for yy in range(NY)
            ).astype(BF16)
            for h in range(HPD):
                fresh[h, first * rows : end * rows] = both[:, h * HD : (h + 1) * HD]

    def attend_keys(h, base, size, with_fresh):
        q = queries[h, pl.ds(base, size)]
        scores = [dot_nt(q, keys[h, c * chunk : (c + 1) * chunk]) for c in range(3)]
        peaks = [jnp.max(s, axis=1, keepdims=True) for s in scores]
        replaced = [patch[0] == y * 3 + c for c in range(3)]
        peaks = [jnp.where(r, NEG_BIG, p) for r, p in zip(replaced, peaks)]
        peak = jnp.maximum(jnp.maximum(peaks[0], peaks[1]), peaks[2])
        if with_fresh:
            fresh_scores = dot_nt(q, fresh_k[h])
            peak = jnp.maximum(peak, jnp.max(fresh_scores, axis=1, keepdims=True))
        total, own = 0.0, 0.0
        for c in range(3):
            w = jnp.exp2((scores[c] - jnp.where(replaced[c], -NEG_BIG, peak)) * SCALE)
            total = total + jnp.sum(w, axis=1, keepdims=True)
            own = own + dot(w.astype(BF16), vals[h, c * chunk : (c + 1) * chunk])
        if with_fresh:
            w = jnp.exp2((fresh_scores - peak) * SCALE)
            total = total + jnp.sum(w, axis=1, keepdims=True)
            own = own + dot(w.astype(BF16), fresh_v[h])
        return peak, total, own

    def attend(g, h_first=0, h_end=HPD):
        base, size = span_of(g)
        if h_first == 0:
            place_queries(g)

        def head(h, _):
            peak, total, own = attend_keys(h, base, size, False)
            acc[h, pl.ds(base, size)] = own
            top[h, pl.ds(base, size)] = jnp.broadcast_to(peak, (size, 128))
            mass[h, pl.ds(base, size)] = jnp.broadcast_to(total, (size, 128))
            return 0

        lax.fori_loop(h_first, h_end, head, 0)

    total_slots = NY * slots
    per_subject = slots // SUBJ

    def attend_guests(g):
        first, end = GROUPS[g]
        mine = (end - first) * rows
        spot = iota((mine, total_slots), 1)
        inside = lax.rem(spot, slots)
        subject = inside // per_subject
        slot_index = spot // slots * per_subject + lax.rem(inside, per_subject)
        live = jnp.zeros((mine, total_slots), jnp.int32)
        for s in range(SUBJ):
            live = jnp.where(subject == s, counts[0, s], live)
        regions = hid[first:end, y, :, width:].reshape(mine, 128).astype(F32)[:, 0:1]
        mask = (regions == (subject + 1).astype(F32)) & (slot_index < live)
        for h in range(HPD):
            own_rows = [queries[h, pl.ds(pl.multiple_of(i * quad + y * rows, rows), rows)] for i in range(first, end)]
            q = jnp.concatenate(own_rows, axis=0)
            g_keys = gk[:, :, h * HD : (h + 1) * HD].reshape(total_slots, HD)
            g_vals = gk[:, :, (HPD + h) * HD : (HPD + h + 1) * HD].reshape(total_slots, HD)
            s = dot_nt(q, g_keys)
            peak = jnp.max(jnp.where(mask, s, NEG_BIG), axis=1, keepdims=True)
            w = jnp.where(mask, jnp.exp2(jnp.where(mask, (s - peak) * SCALE, 0.0)), 0.0)
            total = jnp.maximum(jnp.sum(w, axis=1, keepdims=True), 1.0)
            guest[h, first * rows : end * rows] = dot(w.astype(BF16), g_vals) / total

    def send_group(g, packed_ml):
        first, end = GROUPS[g]
        high = packed_ml.astype(BF16).astype(F32)
        middle = (packed_ml - high).astype(BF16).astype(F32)
        low = packed_ml - high - middle
        spread = high + pltpu.roll(middle, 2 * HPD, 1) + pltpu.roll(low, 4 * HPD, 1)
        po_send[first:end, :, :, HPD * HD :] = spread.astype(BF16).reshape(end - first, NY, rows, 128)
        for j, target in enumerate(peers):
            src = po_send.at[pl.ds(first, end - first), at_y(j + 1)]
            go(remote(src, po.at[y, pl.ds(first, end - first)], po_ss.at[g, j], po_rs.at[g, y], target))
        po[y, first:end] = po_send[first:end, y]

    def pack_ml(packed_ml, h, peak, total, size):
        packed_ml = jnp.where(lane[0:size] == h, peak, packed_ml)
        return jnp.where(lane[0:size] == h + HPD, total, packed_ml)

    def attend_last(g):
        first, end = GROUPS[g]
        base, size = span_of(g)

        packed_ml = jnp.zeros((size, 128), F32)
        for h in range(HPD):
            peak, total, own = attend_keys(h, base, size, True)
            normal = (own / total).astype(BF16)
            po_send[first:end, :, :, h * HD : (h + 1) * HD] = normal.reshape(end - first, NY, rows, HD)
            packed_ml = pack_ml(packed_ml, h, peak, total, size)
        send_group(g, packed_ml)

    def finish_group(g):
        first, end = GROUPS[g]
        base, size = span_of(g)
        packed_ml = jnp.zeros((size, 128), F32)
        for h in range(HPD):
            s = dot_nt(queries[h, pl.ds(base, size)], fresh_k[h])
            old_peak = top[h, pl.ds(base, size)]
            peak = jnp.maximum(jnp.max(s, axis=1, keepdims=True), old_peak)
            w = jnp.exp2((s - jnp.concatenate([peak, peak], axis=1)) * SCALE)
            alpha = jnp.exp2((old_peak - peak) * SCALE)
            total = jnp.sum(w, axis=1, keepdims=True) + alpha * mass[h, pl.ds(base, size)]
            own = (dot(w.astype(BF16), fresh_v[h]) + alpha * acc[h, pl.ds(base, size)]) / total
            po_send[first:end, :, :, h * HD : (h + 1) * HD] = own.astype(BF16).reshape(end - first, NY, rows, HD)
            packed_ml = pack_ml(packed_ml, h, peak, total, size)
        send_group(g, packed_ml)

    def merge(g):
        first, end = GROUPS[g]
        base, size = span_of(g)
        mine = (end - first) * rows
        for j in range(1, NY):
            recv(po.at[at_y(j), pl.ds(first, end - first)], po_rs.at[g, at_y(j)])
        peaks, totals = [], []
        for yy in range(NY):
            spread = po[yy, first:end, :, HPD * HD :].reshape(mine, 128).astype(F32)
            stat = spread + pltpu.roll(spread, 128 - 2 * HPD, 1) + pltpu.roll(spread, 128 - 4 * HPD, 1)
            used = lane[0:mine] < HPD
            peaks.append(jnp.where(used, stat, 0.0))
            totals.append(jnp.where(used, pltpu.roll(stat, 128 - HPD, 1), 1.0))
        peak = jnp.maximum(jnp.maximum(peaks[0], peaks[1]), jnp.maximum(peaks[2], peaks[3]))
        shares = [jnp.exp2((p - peak) * SCALE) * t for p, t in zip(peaks, totals)]
        inverse = 1.0 / (shares[0] + shares[1] + shares[2] + shares[3])
        shares = [share * inverse for share in shares]
        mixed = []
        for h in range(HPD):
            own = sum(
                po[yy, first:end, :, h * HD : (h + 1) * HD].reshape(mine, HD).astype(F32) * shares[yy][:, h : h + 1]
                for yy in range(NY)
            )
            mixed.append((own + guest[h, first * rows : end * rows]).astype(BF16))
        ordered = dot(jnp.concatenate(mixed, axis=1), reorder[...]).astype(BF16)
        tile = 512

        for t in range(width // tile):
            cols = pl.ds(t * tile, tile)
            w = woall[:, :, cols].reshape(NY * block, tile)
            part[first:end, :, cols] = dot(ordered, w).reshape(end - first, rows, tile)

    for yy, what, _, _ in (streams[2], streams[3], streams[1]):
        wait_hid(0, yy, what)
        send_hid(0, yy, what, up, -1)
        send_hid(0, yy, what, down, 1)
    for j, target in enumerate(peers):
        go(remote(gk.at[y], gk.at[y], gk_ss.at[j], gk_rs.at[y], target))
    send_wo(0)
    split_some(0, 4)
    for copy in w_copies:
        copy.wait()
    project(0)

    def late_guests():
        for j in range(1, NY):
            recv(gk.at[at_y(j)], gk_rs.at[at_y(j)])
        attend_guests(0)

    work = {
        (1, 0): [ lambda: split_some(4, 4)],
        (1, 1): [lambda: split_some(8, 4, True)],
        (2, 0): [lambda: project(1)],
        (2, 1): [lambda: attend(0)],
        (2, 3): [lambda: send_wo(1), lambda: attend(1, 0, 2)],
        (3, 0): [lambda: project(2), lambda: attend(1, 2, 3)],
        (3, 1): [late_guests, lambda: attend_guests(1)],
        (3, 2): [lambda: attend(2, 0, 2)],
        (3, 3): [lambda: project(3), pass_wo, lambda: attend(2, 2, 3), lambda: attend_guests(2), lambda: attend(3, 0, 2)],
    }
    for k in range(1, 5):
        before_step = len(sends)
        for i, (yy, what, hops_up, hops_down) in enumerate(streams):
            for sign, hops, onward in ((-1, hops_up, up), (1, hops_down, down)):
                if k > hops:
                    continue
                d = sign * k
                wait_hid(d, yy, part_at(what, k))
                if k == NEAR and what in lateral:
                    wait_hid(d, yy, lateral[what])
                if k < hops:
                    send_hid(d, yy, part_at(what, k + 1), onward, d + sign)
                if k <= NEAR and what == "r":
                    send_hid(d, yy, "c", right, d)
                    send_hid(d, yy, "d", left, d)
            for task in work.get((k, i), ()):
                task()
    project(4)
    drain(20)
    attend(3, 2, 3)
    attend_guests(3)
    place_fresh(0, 4)
    place_fresh(4, 5)
    place_queries(4)
    attend_last(4)
    finish_group(3)
    attend_guests(4)
    drain(6)
    own_wo.wait()
    for j, i in ((1, 0), (2, 0), (2, 1), (3, 1)):
        wait_wo(at_y(j), i)

    wide_tile = width // 4
    cols = [pl.ds(i * wide_tile, wide_tile) for i in range(4)]
    order = ((0, 0), (1, 1), (0, 2), (1, 3), (0, 1), (1, 0), (0, 3), (1, 2))
    for dist in (4, 3, 2, 1):
        merge(dist)
        for d, s in order:
            hops = 4 if d == s % 2 else 3
            if dist > hops:
                continue
            step = 1 if d == 0 else -1
            term = part[SLOT[step * dist], :, cols[s]]
            if dist < hops:
                recv(rs_recv.at[d, s, dist], rs_rs.at[d, s, dist])
                term = term + rs_recv[d, s, dist].astype(F32)
            rs_send[d, s, dist - 1] = term.astype(BF16)
            target = up if d == 0 else down
            n = dist - 1
            go(remote(rs_send.at[d, s, n], rs_recv.at[d, s, n], rs_ss.at[d, s, n], rs_rs.at[d, s, n], target))
        if dist > 1:
            finish_group(dist - 2)
    merge(0)
    for s in (0, 2, 1, 3):
        total = part[0, :, cols[s]]
        for d in range(2):
            recv(rs_recv.at[d, s, 0], rs_rs.at[d, s, 0])
            total = total + rs_recv[d, s, 0].astype(F32)
        gate = modul[2, :, cols[s]]
        res[s] = (act[:, cols[s]].astype(F32) + gate * total).astype(BF16)
        go(remote(res.at[s], out.at[:, cols[s]], res_ss.at[s], res_rs.at[s], (after, u)))
    drain()
    for s in range(4):
        recv(out.at[:, cols[s]], res_rs.at[s])


def shards(
    activations, patch_index, modulation, qkv_weight, out_weight, stale_cache, id_cache, region_ids, id_counts
):
    _, rows, width = activations.shape
    span = stale_cache.shape[2]
    slots = id_cache.shape[2] * id_cache.shape[3]
    line = NZ * rows
    tokens = NY * line
    block = qkv_weight.shape[2] // 3
    dma = pltpu.SemaphoreType.DMA
    vmem = pl.BlockSpec(memory_space=pltpu.VMEM)
    smem = pl.BlockSpec(memory_space=pltpu.SMEM)
    anywhere = pl.BlockSpec(memory_space=pl.ANY)
    result = pl.pallas_call(
        kernel,
        out_shape=jax.ShapeDtypeStruct((rows, width), BF16),
        in_specs=[vmem, vmem, smem, anywhere, anywhere, anywhere, vmem, vmem, smem],
        out_specs=vmem,
        scratch_shapes=[
            pltpu.VMEM((NZ, NY, rows, width + 128), BF16),
            pltpu.VMEM((3 * 128, width), BF16),
            pltpu.VMEM((2, 256, 2, HPD * HD), BF16),
            pltpu.VMEM((HPD, span, HD), BF16),
            pltpu.VMEM((HPD, span, HD), BF16),
            pltpu.VMEM((NZ, NY, rows, 3 * 128), BF16),
            pltpu.VMEM((NY, tokens, 128), BF16),
            pltpu.VMEM((NY, NZ, rows, 256), BF16),
            pltpu.VMEM((HPD, tokens, HD), BF16),
            pltpu.VMEM((HPD, line, HD), BF16),
            pltpu.VMEM((HPD, line, HD), BF16),
            pltpu.VMEM((HPD, tokens, HD), F32),
            pltpu.VMEM((HPD, tokens, 128), F32),
            pltpu.VMEM((HPD, tokens, 128), F32),
            pltpu.VMEM((NZ, NY, rows, (HPD + 1) * HD), BF16),
            pltpu.VMEM((NY, NZ, rows, (HPD + 1) * HD), BF16),
            pltpu.VMEM((HPD, line, HD), F32),
            pltpu.VMEM((NY, slots, 2 * HPD * HD), BF16),
            pltpu.VMEM((NY, block, width), BF16),
            pltpu.VMEM((NZ, rows, width), F32),
            pltpu.VMEM((2, 4, 4, rows, width // 4), BF16),
            pltpu.VMEM((2, 4, 4, rows, width // 4), BF16),
            pltpu.VMEM((4, rows, width // 4), BF16),
            pltpu.VMEM((NY * 128, HPD * HD), BF16),
            pltpu.VMEM((HPD * HD, NY * block), BF16),
            dma((64,)), dma((NZ, NY, 2)),
            dma((5, 3)), dma((5, NY)),
            dma((5, 3)), dma((5, NY)),
            dma((5, 3)), dma((5, NY)),
            dma((3,)), dma((NY,)),
            dma((3, 2)), dma((NY, 2)),
            dma,
            dma((2, 4, 4)), dma((2, 4, 4)),
            dma((4,)), dma((4,)),
            dma((2,)),
            dma((3,)),
        ],
        compiler_params=pltpu.CompilerParams(
            collective_id=0, has_side_effects=True, vmem_limit_bytes=56 * 2**20
        ),
        name="section",
    )(
        activations[0],
        jnp.transpose(modulation, (1, 0, 2)),
        patch_index,
        jnp.swapaxes(qkv_weight[0], 0, 1),
        out_weight[0],
        stale_cache[0, 0],
        id_cache[0, 0].reshape(slots, 2, HPD * HD),
        region_ids,
        id_counts,
    )
    return result[None]


def solution(mesh):
    placed = (
        P("pipe", "ulys", None),
        P("pipe"),
        P("pipe", None, None),
        P("pipe", None, "ulys"),
        P("pipe", "ulys", None),
        P("pipe", "ulys", None, None, None),
        P("pipe", "ulys", None, None, None, None),
        P("pipe", "ulys"),
        P("pipe", None),
    )
    return jax.shard_map(
        shards, mesh=mesh, in_specs=placed, out_specs=P("pipe", "ulys", None), check_vma=False
    )
```

```python
import functools

import jax
import jax.numpy as jnp
from jax import lax
from jax.experimental import pallas as pl
from jax.experimental.pallas import tpu as pltpu
from jax.sharding import PartitionSpec as P

MESH = pl.DeviceIdType.MESH
HD = 128
HPD = 3
NZ = 8
NY = 4
SUBJ = 6
NEG_BIG = -1e30
FACTOR = HD**-0.5
LOG2E = 1.4426950408889634
SCALE = FACTOR * LOG2E
F32 = jnp.float32
BF16 = jnp.bfloat16


def iota(shape, dim):
    return lax.broadcasted_iota(jnp.int32, shape, dim)


def one_hot(cond):
    return jnp.where(cond, 1.0, 0.0).astype(BF16)


def dot_nt(a, b):
    return lax.dot_general(a, b, (((1,), (1,)), ((), ())), preferred_element_type=F32)


def dot(a, b):
    return jnp.dot(a, b, preferred_element_type=F32)


ORDER = (0, -1, 1, -2, 2, -3, 3, 4)
SLOT = {d: i for i, d in enumerate(ORDER)}
SLOT[-4] = SLOT[4]
NEAR = 2
GROUPS = ((0, 1), (1, 3), (3, 5), (5, 7), (7, 8))


def kernel(
    act, modul, patch, wt, wo, cache, ids, region, counts,
    out,
    hid, wts, cbuf, keys, vals, pieces, qx, kvx, queries, fresh_k, fresh_v, acc, top, mass,
    po_send, po, guest, gk, woall, part, rs_send, rs_recv, res, place, reorder,
    hid_ss, hid_rs, q_ss, q_rs, kv_ss, kv_rs, po_ss, po_rs,
    gk_ss, gk_rs, wo_ss, wo_rs, own_sem, rs_ss, rs_rs, res_ss, res_rs, c_sem, w_sem,
):
    pipe = lax.axis_index("pipe")
    u = lax.axis_index("ulys")
    z, y = u // NY, lax.rem(u, NY)
    rows, width = act.shape
    quad = NY * rows
    line = NZ * rows
    split = width // 2
    span = cache.shape[0]
    chunk = span // 3

    def at_y(j):
        return lax.rem(y + j, NY)

    def at_z(k):
        return lax.rem(z + k + NZ, NZ)

    def dev(zz, yy):
        return (pipe, zz * NY + yy)

    after, before = lax.rem(pipe + 1, 8), lax.rem(pipe + 7, 8)
    up, down = dev(at_z(1), y), dev(at_z(-1), y)
    right, far, left = (dev(z, at_y(j)) for j in range(1, NY))
    peers = (right, far, left)

    def remote(src, dst, ss, rs, target):
        return pltpu.make_async_remote_copy(src, dst, ss, rs, target, device_id_type=MESH)

    block = wt.shape[0] // 3
    w_copies = [
        pltpu.make_async_copy(wt.at[pl.ds(i * block, block)], wts.at[pl.ds(i * 128, block)], w_sem.at[i])
        for i in range(3)
    ]
    for copy in w_copies:
        copy.start()

    def cache_copy(i):
        return pltpu.make_async_copy(cache.at[pl.ds(i * 256, 256)], cbuf.at[lax.rem(i, 2)], c_sem.at[lax.rem(i, 2)])

    cache_copy(0).start()
    own_wo = pltpu.make_async_copy(wo, woall.at[y], own_sem)
    own_wo.start()

    barrier = pltpu.get_barrier_semaphore()
    greeted = [right, far, left, up, down, (after, u), (before, u)]
    for target in greeted:
        pl.semaphore_signal(barrier, inc=1, device_id=target, device_id_type=MESH)

    lifted = act[...].astype(F32)
    center = jnp.mean(lifted, axis=1, keepdims=True)
    spread = jnp.mean(jnp.square(lifted - center), axis=1, keepdims=True)
    normed = (lifted - center) * lax.rsqrt(spread + 1e-06)
    hid[0, y, :, 0:width] = (normed * (1.0 + modul[1]) + modul[0]).astype(BF16)
    diagonal = iota((rows, rows), 0) == iota((rows, rows), 1)
    wide = jnp.broadcast_to(region[...].astype(F32), (rows, rows))
    column = jnp.sum(jnp.where(diagonal, wide, 0.0), axis=1, keepdims=True)
    hid[0, y, :, width:] = jnp.broadcast_to(column, (rows, 128)).astype(BF16)

    slots = ids.shape[0]
    packed = ids[...].reshape(2 * slots, HPD * HD)
    pick = iota((slots, 2 * slots), 1) - 2 * iota((slots, 2 * slots), 0)
    gk[y, :, 0 : HPD * HD] = dot(one_hot(pick == 0), packed).astype(BF16)
    gk[y, :, HPD * HD :] = dot(one_hot(pick == 1), packed).astype(BF16)

    pl.semaphore_wait(barrier, len(greeted))

    sends = []

    def go(copy):
        copy.start()
        sends.append(copy)

    def drain(keep=0):
        done = sends[: len(sends) - keep]
        del sends[: len(sends) - keep]
        for copy in done:
            copy.wait_send()

    def recv(ref, rs):
        remote(ref, ref, hid_ss.at[0], rs, dev(z, y)).wait_recv()

    parts = {
        "r": (pl.ds(0, width + 128), 0),
        "w": (pl.ds(0, width), 0),
        "a": (pl.ds(0, split), 0),
        "b": (pl.ds(width - split, split), 0),
        "c": (pl.ds(0, width - split), 1),
        "d": (pl.ds(split, width - split), 1),
    }
    next_send = iter(range(64))

    def send_hid(d, yy, what, target, d_there):
        cols, n = parts[what]
        src, dst = hid.at[SLOT[d], yy, :, cols], hid.at[SLOT[d_there], yy, :, cols]
        go(remote(src, dst, hid_ss.at[next(next_send)], hid_rs.at[SLOT[d_there], yy, n], target))

    def wait_hid(d, yy, what):
        cols, n = parts[what]
        recv(hid.at[SLOT[d], yy, :, cols], hid_rs.at[SLOT[d], yy, n])

    streams = ((y, "r", 4, 3), (at_y(2), "w", 3, 4), (at_y(1), "a", 4, 3), (at_y(3), "b", 3, 4))
    lateral = {"a": "d", "b": "c"}

    def part_at(what, k):
        return "w" if what in lateral and k > NEAR else what

    wo_half = [pl.ds(i * (block // 2), block // 2) for i in range(2)]

    def wait_wo(yy, i):
        recv(woall.at[yy, wo_half[i]], wo_rs.at[yy, i])

    def send_wo(i):
        for j, target in enumerate((right, left)):
            go(remote(wo.at[wo_half[i]], woall.at[y, wo_half[i]], wo_ss.at[j, i], wo_rs.at[y, i], target))

    def pass_wo():
        for i, (yy, target) in enumerate(((at_y(3), right), (at_y(1), left))):
            wait_wo(yy, i)
            ref = woall.at[yy, wo_half[i]]
            go(remote(ref, ref, wo_ss.at[2, i], wo_rs.at[yy, i], target))

    send_hid(0, y, "r", up, -1)
    send_hid(0, y, "r", down, 1)
    for what, target in (("a", left), ("b", right), ("w", far), ("d", left), ("c", right)):
        send_hid(0, y, what, target, 0)

    spot, goal = iota((NY * 128, HPD * HD), 0), iota((NY * 128, HPD * HD), 1)
    inner = lax.rem(spot, 128)
    found = (spot // 128 == lax.rem(goal, 128) // 32) & (inner // 32 == goal // 128)
    place[...] = one_hot(found & (lax.rem(inner, 32) == lax.rem(goal, 32)))
    spot, goal = iota((HPD * HD, NY * block), 0), iota((HPD * HD, NY * block), 1)
    found = (goal // block == lax.rem(spot, HD) // 32) & (lax.rem(goal, block) // 32 == spot // HD)
    reorder[...] = one_hot(found & (lax.rem(goal, 32) == lax.rem(spot, 32)))
    for i in range(3):
        wts[pl.ds(i * 128 + block, 128 - block)] = jnp.zeros((128 - block, width), BF16)

    pick_c = iota((256, 512), 1) - 2 * iota((256, 512), 0)
    even, odd = one_hot(pick_c == 0), one_hot(pick_c == 1)

    def split_cache(i, last):
        if not last:
            cache_copy(i + 1).start()
        cache_copy(i).wait()
        x = cbuf[lax.rem(i, 2)].reshape(512, HPD * HD)
        kk = dot(even, x).astype(BF16)
        vv = dot(odd, x).astype(BF16)
        for h in range(HPD):
            keys[h, pl.ds(pl.multiple_of(i * 256, 256), 256)] = kk[:, h * HD : (h + 1) * HD]
            vals[h, pl.ds(pl.multiple_of(i * 256, 256), 256)] = vv[:, h * HD : (h + 1) * HD]

    def split_some(first, count, last=False):
        def body(i, _):
            split_cache(first + i, False)
            return 0

        lax.fori_loop(0, count - (1 if last else 0), body, 0)
        if last:
            split_cache(jnp.int32(first + count - 1), True)

    def span_of(g):
        first, end = GROUPS[g]
        return first * quad, (end - first) * quad

    def project(g):
        first, end = GROUPS[g]
        for d in ORDER[first:end]:
            if abs(d) < NEAR:
                wait_hid(d, at_y(3), "c")
                wait_hid(d, at_y(1), "d")
        base, size = span_of(g)
        x = hid[first:end, :, :, 0:width].reshape(size, width)
        p = dot_nt(x, wts[...]).astype(BF16)
        pieces[first:end] = p.reshape(end - first, NY, rows, 3 * 128)
        qx[y, pl.ds(base, size)] = p[:, 0:128]
        for j, target in enumerate(peers):
            q = qx.at[y, pl.ds(base, size)]
            go(remote(q, q, q_ss.at[g, j], q_rs.at[g, y], target))
        for j, target in enumerate(peers):
            kv = pieces.at[pl.ds(first, end - first), at_y(j + 1), :, pl.ds(128, 256)]
            go(remote(kv, kvx.at[y, pl.ds(first, end - first)], kv_ss.at[g, j], kv_rs.at[g, y], target))
        kvx[y, first:end] = pieces[first:end, y, :, 128:384]

    lane = iota((256, 128), 1)

    def place_queries(g):
        base, size = span_of(g)
        for j in range(1, NY):
            recv(qx.at[at_y(j), pl.ds(base, size)], q_rs.at[g, at_y(j)])
        full = sum(dot(qx[yy, pl.ds(base, size)], place[yy * 128 : yy * 128 + 128]) for yy in range(NY)).astype(BF16)
        for h in range(HPD):
            queries[h, pl.ds(base, size)] = full[:, h * HD : (h + 1) * HD]

    def place_fresh(g_first, g_end):
        for g in range(g_first, g_end):
            first, end = GROUPS[g]
            for j in range(1, NY):
                recv(kvx.at[at_y(j), pl.ds(first, end - first)], kv_rs.at[g, at_y(j)])
        first, end = GROUPS[g_first][0], GROUPS[g_end - 1][1]
        size = (end - first) * rows
        for s, fresh in enumerate((fresh_k, fresh_v)):
            both = sum(
                dot(kvx[yy, first:end, :, s * 128 : s * 128 + 128].reshape(size, 128), place[yy * 128 : yy * 128 + 128])
                for yy in range(NY)
            ).astype(BF16)
            for h in range(HPD):
                fresh[h, first * rows : end * rows] = both[:, h * HD : (h + 1) * HD]

    def attend_keys(h, base, size, with_fresh):
        q = queries[h, pl.ds(base, size)]
        scores = [dot_nt(q, keys[h, c * chunk : (c + 1) * chunk]) for c in range(3)]
        peaks = [jnp.max(s, axis=1, keepdims=True) for s in scores]
        replaced = [patch[0] == y * 3 + c for c in range(3)]
        peaks = [jnp.where(r, NEG_BIG, p) for r, p in zip(replaced, peaks)]
        peak = jnp.maximum(jnp.maximum(peaks[0], peaks[1]), peaks[2])
        if with_fresh:
            fresh_scores = dot_nt(q, fresh_k[h])
            peak = jnp.maximum(peak, jnp.max(fresh_scores, axis=1, keepdims=True))
        total, own = 0.0, 0.0
        for c in range(3):
            w = jnp.exp2((scores[c] - jnp.where(replaced[c], -NEG_BIG, peak)) * SCALE)
            total = total + jnp.sum(w, axis=1, keepdims=True)
            own = own + dot(w.astype(BF16), vals[h, c * chunk : (c + 1) * chunk])
        if with_fresh:
            w = jnp.exp2((fresh_scores - peak) * SCALE)
            total = total + jnp.sum(w, axis=1, keepdims=True)
            own = own + dot(w.astype(BF16), fresh_v[h])
        return peak, total, own

    def attend(g, h_first=0, h_end=HPD):
        base, size = span_of(g)
        if h_first == 0:
            place_queries(g)

        def head(h, _):
            peak, total, own = attend_keys(h, base, size, False)
            acc[h, pl.ds(base, size)] = own
            top[h, pl.ds(base, size)] = jnp.broadcast_to(peak, (size, 128))
            mass[h, pl.ds(base, size)] = jnp.broadcast_to(total, (size, 128))
            return 0

        lax.fori_loop(h_first, h_end, head, 0)

    total_slots = NY * slots
    per_subject = slots // SUBJ

    def attend_guests(g):
        first, end = GROUPS[g]
        mine = (end - first) * rows
        spot = iota((mine, total_slots), 1)
        inside = lax.rem(spot, slots)
        subject = inside // per_subject
        slot_index = spot // slots * per_subject + lax.rem(inside, per_subject)
        live = jnp.zeros((mine, total_slots), jnp.int32)
        for s in range(SUBJ):
            live = jnp.where(subject == s, counts[0, s], live)
        regions = hid[first:end, y, :, width:].reshape(mine, 128).astype(F32)[:, 0:1]
        mask = (regions == (subject + 1).astype(F32)) & (slot_index < live)
        for h in range(HPD):
            own_rows = [queries[h, pl.ds(pl.multiple_of(i * quad + y * rows, rows), rows)] for i in range(first, end)]
            q = jnp.concatenate(own_rows, axis=0)
            g_keys = gk[:, :, h * HD : (h + 1) * HD].reshape(total_slots, HD)
            g_vals = gk[:, :, (HPD + h) * HD : (HPD + h + 1) * HD].reshape(total_slots, HD)
            s = dot_nt(q, g_keys)
            peak = jnp.max(jnp.where(mask, s, NEG_BIG), axis=1, keepdims=True)
            w = jnp.where(mask, jnp.exp2(jnp.where(mask, (s - peak) * SCALE, 0.0)), 0.0)
            total = jnp.maximum(jnp.sum(w, axis=1, keepdims=True), 1.0)
            guest[h, first * rows : end * rows] = dot(w.astype(BF16), g_vals) / total

    def send_group(g, packed_ml):
        first, end = GROUPS[g]
        high = packed_ml.astype(BF16).astype(F32)
        middle = (packed_ml - high).astype(BF16).astype(F32)
        low = packed_ml - high - middle
        spread = high + pltpu.roll(middle, 2 * HPD, 1) + pltpu.roll(low, 4 * HPD, 1)
        po_send[first:end, :, :, HPD * HD :] = spread.astype(BF16).reshape(end - first, NY, rows, 128)
        for j, target in enumerate(peers):
            src = po_send.at[pl.ds(first, end - first), at_y(j + 1)]
            go(remote(src, po.at[y, pl.ds(first, end - first)], po_ss.at[g, j], po_rs.at[g, y], target))
        po[y, first:end] = po_send[first:end, y]

    def pack_ml(packed_ml, h, peak, total, size):
        packed_ml = jnp.where(lane[0:size] == h, peak, packed_ml)
        return jnp.where(lane[0:size] == h + HPD, total, packed_ml)

    def attend_last(g):
        first, end = GROUPS[g]
        base, size = span_of(g)

        packed_ml = jnp.zeros((size, 128), F32)
        for h in range(HPD):
            peak, total, own = attend_keys(h, base, size, True)
            normal = (own / total).astype(BF16)
            po_send[first:end, :, :, h * HD : (h + 1) * HD] = normal.reshape(end - first, NY, rows, HD)
            packed_ml = pack_ml(packed_ml, h, peak, total, size)
        send_group(g, packed_ml)

    def finish_group(g):
        first, end = GROUPS[g]
        base, size = span_of(g)
        packed_ml = jnp.zeros((size, 128), F32)
        for h in range(HPD):
            s = dot_nt(queries[h, pl.ds(base, size)], fresh_k[h])
            old_peak = top[h, pl.ds(base, size)]
            peak = jnp.maximum(jnp.max(s, axis=1, keepdims=True), old_peak)
            w = jnp.exp2((s - jnp.concatenate([peak, peak], axis=1)) * SCALE)
            alpha = jnp.exp2((old_peak - peak) * SCALE)
            total = jnp.sum(w, axis=1, keepdims=True) + alpha * mass[h, pl.ds(base, size)]
            own = (dot(w.astype(BF16), fresh_v[h]) + alpha * acc[h, pl.ds(base, size)]) / total
            po_send[first:end, :, :, h * HD : (h + 1) * HD] = own.astype(BF16).reshape(end - first, NY, rows, HD)
            packed_ml = pack_ml(packed_ml, h, peak, total, size)
        send_group(g, packed_ml)

    def merge(g):
        first, end = GROUPS[g]
        base, size = span_of(g)
        mine = (end - first) * rows
        for j in range(1, NY):
            recv(po.at[at_y(j), pl.ds(first, end - first)], po_rs.at[g, at_y(j)])
        peaks, totals = [], []
        for yy in range(NY):
            spread = po[yy, first:end, :, HPD * HD :].reshape(mine, 128).astype(F32)
            stat = spread + pltpu.roll(spread, 128 - 2 * HPD, 1) + pltpu.roll(spread, 128 - 4 * HPD, 1)
            used = lane[0:mine] < HPD
            peaks.append(jnp.where(used, stat, 0.0))
            totals.append(jnp.where(used, pltpu.roll(stat, 128 - HPD, 1), 1.0))
        peak = jnp.maximum(jnp.maximum(peaks[0], peaks[1]), jnp.maximum(peaks[2], peaks[3]))
        shares = [jnp.exp2((p - peak) * SCALE) * t for p, t in zip(peaks, totals)]
        inverse = 1.0 / (shares[0] + shares[1] + shares[2] + shares[3])
        shares = [share * inverse for share in shares]
        mixed = []
        for h in range(HPD):
            own = sum(
                po[yy, first:end, :, h * HD : (h + 1) * HD].reshape(mine, HD).astype(F32) * shares[yy][:, h : h + 1]
                for yy in range(NY)
            )
            mixed.append((own + guest[h, first * rows : end * rows]).astype(BF16))
        ordered = dot(jnp.concatenate(mixed, axis=1), reorder[...]).astype(BF16)
        tile = 512

        for t in range(width // tile):
            cols = pl.ds(t * tile, tile)
            w = woall[:, :, cols].reshape(NY * block, tile)
            part[first:end, :, cols] = dot(ordered, w).reshape(end - first, rows, tile)

    for yy, what, _, _ in (streams[2], streams[3], streams[1]):
        wait_hid(0, yy, what)
        send_hid(0, yy, what, up, -1)
        send_hid(0, yy, what, down, 1)
    for j, target in enumerate(peers):
        go(remote(gk.at[y], gk.at[y], gk_ss.at[j], gk_rs.at[y], target))
    send_wo(0)
    split_some(0, 4)
    for copy in w_copies:
        copy.wait()
    project(0)

    def late_guests():
        for j in range(1, NY):
            recv(gk.at[at_y(j)], gk_rs.at[at_y(j)])
        attend_guests(0)

    work = {
        (1, 0): [ lambda: split_some(4, 4)],
        (1, 1): [lambda: split_some(8, 4, True)],
        (2, 0): [lambda: project(1)],
        (2, 1): [lambda: attend(0)],
        (2, 3): [lambda: attend(1, 0, 2)],
        (3, 0): [lambda: project(2), lambda: send_wo(1), lambda: attend(1, 2, 3)],
        (3, 1): [late_guests, lambda: attend_guests(1)],
        (3, 2): [lambda: attend(2, 0, 2)],
        (3, 3): [lambda: project(3), lambda: attend(2, 2, 3), lambda: attend_guests(2), lambda: attend(3, 0, 2)],
    }
    for k in range(1, 5):
        before_step = len(sends)
        for i, (yy, what, hops_up, hops_down) in enumerate(streams):
            for sign, hops, onward in ((-1, hops_up, up), (1, hops_down, down)):
                if k > hops:
                    continue
                d = sign * k
                wait_hid(d, yy, part_at(what, k))
                if k == NEAR and what in lateral:
                    wait_hid(d, yy, lateral[what])
                if k < hops:
                    send_hid(d, yy, part_at(what, k + 1), onward, d + sign)
                if k <= NEAR and what == "r":
                    send_hid(d, yy, "c", right, d)
                    send_hid(d, yy, "d", left, d)
            for task in work.get((k, i), ()):
                task()
    project(4)
    pass_wo()
    drain(20)
    attend(3, 2, 3)
    attend_guests(3)
    place_fresh(0, 4)
    place_fresh(4, 5)
    place_queries(4)
    attend_last(4)
    finish_group(3)
    attend_guests(4)
    drain(6)
    own_wo.wait()
    for j, i in ((1, 0), (2, 0), (2, 1), (3, 1)):
        wait_wo(at_y(j), i)

    wide_tile = width // 4
    cols = [pl.ds(i * wide_tile, wide_tile) for i in range(4)]
    order = ((0, 0), (1, 1), (0, 2), (1, 3), (0, 1), (1, 0), (0, 3), (1, 2))
    for dist in (4, 3, 2, 1):
        merge(dist)
        for d, s in order:
            hops = 4 if d == s % 2 else 3
            if dist > hops:
                continue
            step = 1 if d == 0 else -1
            term = part[SLOT[step * dist], :, cols[s]]
            if dist < hops:
                recv(rs_recv.at[d, s, dist], rs_rs.at[d, s, dist])
                term = term + rs_recv[d, s, dist].astype(F32)
            rs_send[d, s, dist - 1] = term.astype(BF16)
            target = up if d == 0 else down
            n = dist - 1
            go(remote(rs_send.at[d, s, n], rs_recv.at[d, s, n], rs_ss.at[d, s, n], rs_rs.at[d, s, n], target))
        if dist > 1:
            finish_group(dist - 2)
    merge(0)
    for s in (0, 2, 1, 3):
        total = part[0, :, cols[s]]
        for d in range(2):
            recv(rs_recv.at[d, s, 0], rs_rs.at[d, s, 0])
            total = total + rs_recv[d, s, 0].astype(F32)
        gate = modul[2, :, cols[s]]
        res[s] = (act[:, cols[s]].astype(F32) + gate * total).astype(BF16)
        go(remote(res.at[s], out.at[:, cols[s]], res_ss.at[s], res_rs.at[s], (after, u)))
    drain()
    for s in range(4):
        recv(out.at[:, cols[s]], res_rs.at[s])


def shards(
    activations, patch_index, modulation, qkv_weight, out_weight, stale_cache, id_cache, region_ids, id_counts
):
    _, rows, width = activations.shape
    span = stale_cache.shape[2]
    slots = id_cache.shape[2] * id_cache.shape[3]
    line = NZ * rows
    tokens = NY * line
    block = qkv_weight.shape[2] // 3
    dma = pltpu.SemaphoreType.DMA
    vmem = pl.BlockSpec(memory_space=pltpu.VMEM)
    smem = pl.BlockSpec(memory_space=pltpu.SMEM)
    anywhere = pl.BlockSpec(memory_space=pl.ANY)
    result = pl.pallas_call(
        kernel,
        out_shape=jax.ShapeDtypeStruct((rows, width), BF16),
        in_specs=[vmem, vmem, smem, anywhere, anywhere, anywhere, vmem, vmem, smem],
        out_specs=vmem,
        scratch_shapes=[
            pltpu.VMEM((NZ, NY, rows, width + 128), BF16),
            pltpu.VMEM((3 * 128, width), BF16),
            pltpu.VMEM((2, 256, 2, HPD * HD), BF16),
            pltpu.VMEM((HPD, span, HD), BF16),
            pltpu.VMEM((HPD, span, HD), BF16),
            pltpu.VMEM((NZ, NY, rows, 3 * 128), BF16),
            pltpu.VMEM((NY, tokens, 128), BF16),
            pltpu.VMEM((NY, NZ, rows, 256), BF16),
            pltpu.VMEM((HPD, tokens, HD), BF16),
            pltpu.VMEM((HPD, line, HD), BF16),
            pltpu.VMEM((HPD, line, HD), BF16),
            pltpu.VMEM((HPD, tokens, HD), F32),
            pltpu.VMEM((HPD, tokens, 128), F32),
            pltpu.VMEM((HPD, tokens, 128), F32),
            pltpu.VMEM((NZ, NY, rows, (HPD + 1) * HD), BF16),
            pltpu.VMEM((NY, NZ, rows, (HPD + 1) * HD), BF16),
            pltpu.VMEM((HPD, line, HD), F32),
            pltpu.VMEM((NY, slots, 2 * HPD * HD), BF16),
            pltpu.VMEM((NY, block, width), BF16),
            pltpu.VMEM((NZ, rows, width), F32),
            pltpu.VMEM((2, 4, 4, rows, width // 4), BF16),
            pltpu.VMEM((2, 4, 4, rows, width // 4), BF16),
            pltpu.VMEM((4, rows, width // 4), BF16),
            pltpu.VMEM((NY * 128, HPD * HD), BF16),
            pltpu.VMEM((HPD * HD, NY * block), BF16),
            dma((64,)), dma((NZ, NY, 2)),
            dma((5, 3)), dma((5, NY)),
            dma((5, 3)), dma((5, NY)),
            dma((5, 3)), dma((5, NY)),
            dma((3,)), dma((NY,)),
            dma((3, 2)), dma((NY, 2)),
            dma,
            dma((2, 4, 4)), dma((2, 4, 4)),
            dma((4,)), dma((4,)),
            dma((2,)),
            dma((3,)),
        ],
        compiler_params=pltpu.CompilerParams(
            collective_id=0, has_side_effects=True, vmem_limit_bytes=56 * 2**20
        ),
        name="section",
    )(
        activations[0],
        jnp.transpose(modulation, (1, 0, 2)),
        patch_index,
        jnp.swapaxes(qkv_weight[0], 0, 1),
        out_weight[0],
        stale_cache[0, 0],
        id_cache[0, 0].reshape(slots, 2, HPD * HD),
        region_ids,
        id_counts,
    )
    return result[None]


def solution(mesh):
    placed = (
        P("pipe", "ulys", None),
        P("pipe"),
        P("pipe", None, None),
        P("pipe", None, "ulys"),
        P("pipe", "ulys", None),
        P("pipe", "ulys", None, None, None),
        P("pipe", "ulys", None, None, None, None),
        P("pipe", "ulys"),
        P("pipe", None),
    )
    return jax.shard_map(
        shards, mesh=mesh, in_specs=placed, out_specs=P("pipe", "ulys", None), check_vma=False
    )
```
